32 devices in a mesh: wide: 8 (over y, x, core), narrow: 4 (over z).
Axes of the slice: x: 2, y: 2, z: 4, core: 2. Of those that a mesh axis runs over, the one named last changes fastest.
Arguments:
- wavefunction: float32 [2, 512, 512, 256], P(None, 'wide', 'narrow'), may hold values from -6 to 6
- previous_slope: float32 [2, 512, 512, 256], P(None, 'wide', 'narrow'), may hold values from -6 to 6
- potential: float32 [512, 512, 256], P('wide', 'narrow'), may hold values from 0.5 to 3
- kinetic_one: float32 [512, 512], replicated, as said below
- coupling_one: float32 [512, 512], replicated, as said below
- kinetic_two: float32 [512, 512], P('narrow'), as said below
- coupling_two: float32 [512, 512], P('narrow'), as said below
- kinetic_three: float32 [256, 256], replicated, as said below
- coupling_three: float32 [256, 256], replicated, as said below
Outputs:
- slope: float32 [2, 512, 512, 256], P(None, 'wide', 'narrow')
- next_input: float32 [2, 512, 512, 256], P(None, 'wide', 'narrow')
The draws below stay inside these ranges and needn't reach their ends.
Inputs may be any that keep to these rules, and one draw needn't show every extreme that they name: kinetic_one is symmetric. coupling_one is symmetric. kinetic_two is symmetric. coupling_two is symmetric. kinetic_three is symmetric. coupling_three is symmetric.
All inputs are finite; a program needn't handle non-finite values.
Results may differ from the reference program's by a relative error of at most 0.00005.
Values sent between devices are 32-bit elements; how exact they have to be, the bound alone decides.
A program may use at most 384 MiB of HBM per device.

```python
import jax
import jax.numpy as jnp
from jax import lax

N1 = 512
N2 = 512
N3 = 256


def symmetric_matrix(key, order):
    values = jax.random.normal(key, (order, order), jnp.float32)
    return (values + values.T) * (1.0 / jnp.sqrt(2.0 * order))


def draw_kinetic_one(key, part):
    return symmetric_matrix(jax.random.fold_in(key, 11), N1)


def draw_coupling_one(key, part):
    return symmetric_matrix(jax.random.fold_in(key, 12), N1)


def draw_kinetic_two(key, part):
    return symmetric_matrix(jax.random.fold_in(key, 13), N2)


def draw_coupling_two(key, part):
    return symmetric_matrix(jax.random.fold_in(key, 14), N2)


def draw_kinetic_three(key, part):
    return symmetric_matrix(jax.random.fold_in(key, 15), N3)


def draw_coupling_three(key, part):
    return symmetric_matrix(jax.random.fold_in(key, 16), N3)


def steps_of(key, dims, split, least, largest):
    level = 1.0
    for position, shards_of in split:
        steps = jax.random.uniform(jax.random.fold_in(jax.random.fold_in(key, 6), position), (shards_of,), jnp.float32, least / len(split), largest / len(split))
        level = level * jnp.repeat(jnp.exp(steps), dims[position] // shards_of).reshape((-1,) + (1,) * (len(dims) - 1 - position))
    return level


def bell_draw(key, dims, width, limit, cuts=(), held_as=jnp.bfloat16):
    level = steps_of(key, dims, cuts, -0.22, 0.18) if cuts else 1.0
    result = jax.random.normal(key, dims, jnp.float32) * width * level
    return jnp.minimum(jnp.maximum(result, -limit), limit).astype(held_as)


def setup_inputs(seed: int = 0) -> dict:
    seeds = jax.random.split(jax.random.key(seed), 10)
    wavefunction = bell_draw(seeds[0], (2, N1, N2, N3), 1.0, 6.0, ((1, 8), (2, 4)), jnp.float32)
    previous_slope = bell_draw(seeds[1], (2, N1, N2, N3), 1.0, 6.0, ((1, 8), (2, 4)), jnp.float32)
    potential = jnp.clip(0.5 + 2.5 * jax.random.uniform(seeds[2], (N1, N2, N3), jnp.float32) ** steps_of(seeds[2], (N1, N2, N3), ((0, 8), (1, 4)), -0.2, 0.2), 0.5, 3.0)
    kinetic_one = draw_kinetic_one(jax.random.fold_in(seeds[9], 71), 0)
    coupling_one = draw_coupling_one(jax.random.fold_in(seeds[9], 71), 0)
    kinetic_two = draw_kinetic_two(jax.random.fold_in(seeds[9], 71), 0)
    coupling_two = draw_coupling_two(jax.random.fold_in(seeds[9], 71), 0)
    kinetic_three = draw_kinetic_three(jax.random.fold_in(seeds[9], 71), 0)
    coupling_three = draw_coupling_three(jax.random.fold_in(seeds[9], 71), 0)
    return dict(wavefunction=wavefunction, previous_slope=previous_slope, potential=potential, kinetic_one=kinetic_one, coupling_one=coupling_one, kinetic_two=kinetic_two, coupling_two=coupling_two, kinetic_three=kinetic_three, coupling_three=coupling_three)


half_step = 0.1


def along_one(matrix, field):
    return jnp.einsum("ij,cjkl->cikl", matrix, field, precision=lax.Precision.HIGHEST)


def along_two(matrix, field):
    return jnp.einsum("ij,ckjl->ckil", matrix, field, precision=lax.Precision.HIGHEST)


def along_three(matrix, field):
    return jnp.einsum("ij,cklj->ckli", matrix, field, precision=lax.Precision.HIGHEST)


def reference(wavefunction, previous_slope, potential, kinetic_one, coupling_one, kinetic_two, coupling_two, kinetic_three, coupling_three):
    section_in = wavefunction + half_step * previous_slope
    hamil = along_one(kinetic_one, section_in)
    hamil = hamil + along_two(kinetic_two, section_in)
    hamil = hamil + along_three(kinetic_three, section_in)
    coupled = along_one(coupling_one, along_two(coupling_two, along_three(coupling_three, section_in)))
    hamil = hamil + coupled + potential[None] * section_in
    slope = jnp.stack([hamil[1], -hamil[0]])
    next_input = wavefunction + half_step * slope
    return (slope, next_input)
```

```python
import functools

import jax
import jax.numpy as jnp
from jax import lax
from jax.experimental import pallas as pl
from jax.experimental.pallas import tpu as pltpu
from jax.sharding import PartitionSpec as P

half_step = 0.1
MESH = pl.DeviceIdType.MESH
OWN, END, FWD, YROW, WROW, PSI, PHI, SUM_O, SUM_F, YEND = range(10)
TO_S1, BACK_C, BACK_K, TO_S0, TO_W0, BACK_0 = range(6)
BUFFERS = (
    "end0", "other0", "far0", "y0", "w0", "sy", "sw",
    "s0b", "t0", "w0b", "tw", "r0", "b0",
    "s1b", "t1", "rc", "rk", "bc", "bk", "phi",
    "psie", "phie", "po", "pe", "ao", "af", "ba0", "ba1", "se", "y1", "base1", "h0",
)
WIDE_SHAPED = ("t0", "tw", "r0", "t1", "rc", "rk")
SECOND_FIRST = ("s0b", "w0b", "b0", "s1b", "bc", "bk")


def halves(x):
    high = x.astype(jnp.bfloat16)
    return high, (x - high.astype(jnp.float32)).astype(jnp.bfloat16)


def dot3(ah, al, bh, bl):
    dot = functools.partial(jnp.dot, preferred_element_type=jnp.float32)
    return dot(ah, bh) + dot(ah, bl) + dot(al, bh)


def kernel(wide, s, pot, w, wt, k1, c1, k3, c3, *refs):
    buf = dict(zip(BUFFERS, refs[:len(BUFFERS)]))
    (wh, wl, wth, wtl, k1h, k1l, c1h, c1l, k3h, k3l, c3h, c3l, fh, fl, gather,
     zs, zr, ws, wr, wloc) = refs[len(BUFFERS):]
    rows, second, third = s.shape[1:]
    full = rows * wide
    q = second // wide
    step = 8
    nc = rows // step
    me = lax.axis_index("wide")
    z = lax.axis_index("narrow")
    hub = jnp.logical_or(z == 1, z == 2)
    end = jnp.where(z == 1, 0, 3)
    other = 3 - z
    far = 3 - end
    my_hub = jnp.where(z == 0, 1, 2)
    s0, s1 = s.at[0], s.at[1]

    def peer_of(d):
        return lax.rem(me + d, wide)

    barrier = pltpu.get_barrier_semaphore()

    def greet(d, carry):
        pl.semaphore_signal(barrier, inc=1, device_id={"wide": peer_of(d)}, device_id_type=MESH)
        return carry

    lax.fori_loop(1, wide, greet, 0)

    @pl.when(hub)
    def _():
        pl.semaphore_signal(barrier, inc=1, device_id={"narrow": end}, device_id_type=MESH)
        pl.semaphore_signal(barrier, inc=1, device_id={"narrow": other}, device_id_type=MESH)
        pl.semaphore_wait(barrier, wide + 1)

    @pl.when(jnp.logical_not(hub))
    def _():
        pl.semaphore_signal(barrier, inc=1, device_id={"narrow": my_hub}, device_id_type=MESH)
        pl.semaphore_wait(barrier, wide)

    def piece(ref, c):
        return ref.at[pl.ds(pl.multiple_of(c * step, step), step)]

    def zcopy(kind, c, src, dst, target):
        return pltpu.make_async_remote_copy(
            src_ref=piece(src, c), dst_ref=piece(dst, c), send_sem=zs.at[kind, c], recv_sem=zr.at[kind, c],
            device_id={"narrow": target}, device_id_type=MESH)

    def zrecv(kind, c, dst):
        pltpu.make_async_copy(piece(dst, c), piece(dst, c), zr.at[kind, c]).wait()

    def zsent(kind, c, src):
        pltpu.make_async_copy(piece(src, c), piece(src, c), zs.at[kind, c]).wait()

    def each_chunk(f):
        def body(c, carry):
            f(c)
            return carry
        lax.fori_loop(0, nc, body, 0)

    def mine_of(ref, index, size):
        return ref.at[:, pl.ds(pl.multiple_of(index * size, size), size)]

    def to_whole(kind, src, dst):
        def send(d, carry):
            p = peer_of(d)
            pltpu.make_async_remote_copy(
                src_ref=src.at[pl.ds(p * q, q)], dst_ref=mine_of(dst, me, rows),
                send_sem=ws.at[kind], recv_sem=wr.at[kind], device_id={"wide": p}, device_id_type=MESH).start()
            return carry
        lax.fori_loop(1, wide, send, 0)
        pltpu.make_async_copy(src.at[pl.ds(me * q, q)], mine_of(dst, me, rows), wloc.at[kind]).start()

    def to_whole_wait(kind, dst):
        part = dst.at[:, pl.ds(0, (wide - 1) * rows)]
        pltpu.make_async_copy(part, part, wr.at[kind]).wait()
        own = dst.at[:, pl.ds(0, rows)]
        pltpu.make_async_copy(own, own, wloc.at[kind]).wait()

    def from_whole(kind, src, dst):
        def send(d, carry):
            p = peer_of(d)
            pltpu.make_async_remote_copy(
                src_ref=mine_of(src, p, rows), dst_ref=dst.at[pl.ds(me * q, q)],
                send_sem=ws.at[kind], recv_sem=wr.at[kind], device_id={"wide": p}, device_id_type=MESH).start()
            return carry
        lax.fori_loop(1, wide, send, 0)
        pltpu.make_async_copy(mine_of(src, me, rows), dst.at[pl.ds(me * q, q)], wloc.at[kind]).start()

    def from_whole_wait(kind, dst):
        part = dst.at[pl.ds(0, (wide - 1) * q)]
        pltpu.make_async_copy(part, part, wr.at[kind]).wait()
        own = dst.at[pl.ds(0, q)]
        pltpu.make_async_copy(own, own, wloc.at[kind]).wait()

    def wide_sent(kind, src):
        part = src.at[pl.ds(0, (wide - 1) * q)] if src.shape[0] == second else src.at[:, pl.ds(0, (wide - 1) * rows)]
        pltpu.make_async_copy(part, part, ws.at[kind]).wait()

    by_first = pl.BlockSpec((step, second, third), lambda i: (i, 0, 0))
    by_second = pl.BlockSpec((second, step, third), lambda i: (0, i, 0))
    one_row = pl.BlockSpec((1, second, third), lambda i: (i, 0, 0))
    one_whole = pl.BlockSpec((1, full, third), lambda i: (i, 0, 0))

    def swapped(src_ref, g):
        return jnp.swapaxes(src_ref[:, 8 * g:8 * g + 8, :], 0, 1)

    def transpose_stage(src, dst):
        def body(x, out):
            for g in range(second // 8):
                out[8 * g:8 * g + 8, :, :] = jnp.swapaxes(x[:, 8 * g:8 * g + 8, :], 0, 1)
        pltpu.emit_pipeline(body, grid=(nc,), in_specs=[by_first], out_specs=[by_second])(src, dst)

    def third_dot(x, mh, ml):
        xh, xl = halves(x)
        return dot3(xh, xl, mh[...], ml[...])

    group = 32

    def phi_stage(src, dst):
        def body(x, out):
            for g in range(second // group):
                block = x[group * g:group * (g + 1)].reshape(group * step, third)
                result = third_dot(block, c3h, c3l).reshape(group, step, third)
                out[:, group * g:group * (g + 1), :] = jnp.swapaxes(result, 0, 1)
        pltpu.emit_pipeline(body, grid=(nc,), in_specs=[by_second], out_specs=[by_first])(src, dst)

    def coupled_stage(src, dst):
        def body(x, out):
            for g in range(second // group):
                block = x[:, group * g:group * (g + 1), :].reshape(group * step, third)
                result = third_dot(block, c3h, c3l).reshape(step, group, third)
                out[group * g:group * (g + 1), :, :] = jnp.swapaxes(result, 0, 1)
        pltpu.emit_pipeline(body, grid=(nc,), in_specs=[by_first], out_specs=[by_second])(src, dst)

    def base_stage(field, returned, dst, extra=None):
        def body(x, v, back, *rest):
            out = rest[-1]
            for g in range(second // group):
                cut = slice(group * g, group * (g + 1))
                block = x[:, cut, :].reshape(group * step, third)
                result = third_dot(block, k3h, k3l).reshape(step, group, third)
                result = result + v[:, cut, :] * x[:, cut, :] + jnp.swapaxes(back[cut], 0, 1)
                if extra is not None:
                    result = result + rest[0][:, cut, :]
                out[:, cut, :] = result
        ins = [field, pot, returned] + ([] if extra is None else [extra])
        specs = [by_first, by_first, by_second] + ([] if extra is None else [by_first])
        pltpu.emit_pipeline(body, grid=(nc,), in_specs=specs, out_specs=[by_first])(*ins, dst)

    def first_stage(terms, dst):
        def body(*args):
            out = args[-1]
            total = None
            for (_, mh, ml), x in zip(terms, args[:-1]):
                xh, xl = halves(x[0])
                value = dot3(mh[...], ml[...], xh, xl)
                total = value if total is None else total + value
            out[0] = total
        pltpu.emit_pipeline(body, grid=(q,), in_specs=[one_whole] * len(terms), out_specs=[one_whole])(
            *[t[0] for t in terms], dst)

    def place(slot, x):
        at = pl.ds(pl.multiple_of(slot * second, second), second)
        high, low = halves(x)
        fh[at, :] = high
        fl[at, :] = low

    def gather_stage(c):
        def body(own, e, o, f, y, v, ye, ve):
            place(z, own[0])
            place(end, e[0])
            place(other, o[0])
            place(far, f[0])
            for n, out in enumerate((y, ye, v, ve)):
                cut = slice(n * second, (n + 1) * second)
                out[0] = dot3(wh[cut, :], wl[cut, :], fh[...], fl[...])
        pltpu.emit_pipeline(body, grid=(step,), in_specs=[one_row] * 4, out_specs=[one_row] * 4)(
            piece(s0, c), piece(buf["end0"], c), piece(buf["other0"], c), piece(buf["far0"], c),
            piece(buf["y0"], c), piece(buf["w0"], c), piece(buf["sy"], c), piece(buf["sw"], c))

    def scatter_stage(c):
        def body(own, e, pown, pend, yo, ye, ao, af):
            place(0, own[0])
            place(1, e[0])
            place(2, pown[0])
            place(3, pend[0])
            for n in range(4):
                cut = slice(n * second, (n + 1) * second)
                gather[n] = dot3(wth[cut, :], wtl[cut, :], fh[...], fl[...])
            yo[0] = gather[z]
            ye[0] = gather[end]
            ao[0] = gather[other]
            af[0] = gather[far]
        pltpu.emit_pipeline(body, grid=(step,), in_specs=[one_row] * 4, out_specs=[one_row] * 4)(
            piece(s1, c), piece(buf["psie"], c), piece(buf["phi"], c), piece(buf["phie"], c),
            piece(buf["po"], c), piece(buf["pe"], c), piece(buf["ao"], c), piece(buf["af"], c))

    def finish_stage(c):
        def body(po, pe, a0, a1, y, ye):
            y[...] = po[...] + a0[...]
            ye[...] = pe[...] + a1[...]
        two = pl.BlockSpec((2, second, third), lambda i: (i, 0, 0))
        pltpu.emit_pipeline(body, grid=(step // 2,), in_specs=[two] * 4, out_specs=[two] * 2)(
            piece(buf["po"], c), piece(buf["pe"], c), piece(buf["ba0"], c), piece(buf["ba1"], c),
            piece(buf["y1"], c), piece(buf["se"], c))

    @pl.when(hub)
    def _():
        for c in range(min(2, nc)):
            zcopy(OWN, c, s0, buf["other0"], other).start()

    @pl.when(jnp.logical_not(hub))
    def _():
        each_chunk(lambda c: zcopy(END, c, s0, buf["end0"], my_hub).start())

    transpose_stage(s1, buf["s1b"])
    to_whole(TO_S1, buf["s1b"], buf["t1"])
    for matrix, high, low in ((c1, c1h, c1l), (c3, c3h, c3l), (w, wh, wl), (wt, wth, wtl), (k1, k1h, k1l), (k3, k3h, k3l)):
        high[...], low[...] = halves(matrix[...])

    first_at = min(3, nc - 1)
    phi_at = min(5, nc - 1)
    base_at = nc
    coupled_at = nc + 1
    second_at = min(nc + 4, 2 * nc)
    last_at = max(2 * nc - 1, second_at)
    early = nc // 2

    def body(t, carry):
        @pl.when(jnp.logical_and(hub, t + 2 < nc))
        def _():
            zcopy(OWN, t + 2, s0, buf["other0"], other).start()

        @pl.when(jnp.logical_and(hub, t < nc))
        def _():
            zrecv(END, t, buf["end0"])
            zcopy(FWD, t, buf["end0"], buf["far0"], other).start()

        @pl.when(t == first_at)
        def _():
            to_whole_wait(TO_S1, buf["t1"])
            first_stage([(buf["t1"], c1h, c1l)], buf["rc"])
            from_whole(BACK_C, buf["rc"], buf["bc"])

            @pl.when(jnp.logical_not(hub))
            def _():
                for c in range(early):
                    zcopy(PSI, c, s1, buf["psie"], my_hub).start()
            first_stage([(buf["t1"], k1h, k1l)], buf["rk"])
            transpose_stage(s0, buf["s0b"])

        @pl.when(t == phi_at)
        def _():
            from_whole_wait(BACK_C, buf["bc"])
            phi_stage(buf["bc"], buf["phi"])

            @pl.when(jnp.logical_not(hub))
            def _():
                for c in range(nc):
                    if c >= early:
                        zcopy(PSI, c, s1, buf["psie"], my_hub).start()
                    zcopy(PHI, c, buf["phi"], buf["phie"], my_hub).start()
            from_whole(BACK_K, buf["rk"], buf["bk"])
            to_whole(TO_S0, buf["s0b"], buf["t0"])

        @pl.when(jnp.logical_and(hub, jnp.logical_and(t >= nc - 1, t <= 2 * nc - 2)))
        def _():
            c = t - (nc - 1)
            zrecv(PSI, c, buf["psie"])
            zrecv(PHI, c, buf["phie"])
            scatter_stage(c)
            zcopy(SUM_O, c, buf["ao"], buf["ba0"], other).start()
            zcopy(SUM_F, c, buf["af"], buf["ba1"], other).start()

        @pl.when(jnp.logical_and(hub, jnp.logical_and(t >= 1, t <= nc)))
        def _():
            c = t - 1
            zrecv(OWN, c, buf["other0"])
            zrecv(FWD, c, buf["far0"])
            gather_stage(c)
            zcopy(WROW, c, buf["sw"], buf["w0"], end).start()
            zcopy(YROW, c, buf["sy"], buf["y0"], end).start()

        @pl.when(jnp.logical_and(hub, t >= nc + 1))
        def _():
            c = t - (nc + 1)
            zrecv(SUM_O, c, buf["ba0"])
            zrecv(SUM_F, c, buf["ba1"])
            finish_stage(c)
            zcopy(YEND, c, buf["se"], buf["y1"], end).start()

        @pl.when(t == base_at)
        def _():
            from_whole_wait(BACK_K, buf["bk"])
            base_stage(s1, buf["bk"], buf["base1"])

        @pl.when(t == coupled_at)
        def _():
            @pl.when(jnp.logical_not(hub))
            def _():
                each_chunk(lambda c: zrecv(WROW, c, buf["w0"]))
            coupled_stage(buf["w0"], buf["w0b"])
            to_whole(TO_W0, buf["w0b"], buf["tw"])

        @pl.when(t == second_at)
        def _():
            to_whole_wait(TO_S0, buf["t0"])
            to_whole_wait(TO_W0, buf["tw"])
            first_stage([(buf["t0"], k1h, k1l), (buf["tw"], c1h, c1l)], buf["r0"])
            from_whole(BACK_0, buf["r0"], buf["b0"])

        @pl.when(t == last_at)
        def _():
            @pl.when(jnp.logical_not(hub))
            def _():
                each_chunk(lambda c: zrecv(YROW, c, buf["y0"]))
            from_whole_wait(BACK_0, buf["b0"])
            base_stage(s0, buf["b0"], buf["h0"], buf["y0"])
        return carry

    lax.fori_loop(0, 2 * nc + 1, body, 0)

    @pl.when(hub)
    def _():
        def sent(c):
            for kind, name in ((OWN, "s"), (FWD, "end0"), (YROW, "sy"), (WROW, "sw"), (SUM_O, "ao"), (SUM_F, "af"), (YEND, "se")):
                zsent(kind, c, s0 if name == "s" else buf[name])
        each_chunk(sent)

    @pl.when(jnp.logical_not(hub))
    def _():
        def sent(c):
            zsent(END, c, s0)
            zsent(PSI, c, s1)
            zsent(PHI, c, buf["phi"])
            zrecv(YEND, c, buf["y1"])
        each_chunk(sent)

    for kind, name in ((TO_S1, "s1b"), (BACK_C, "rc"), (BACK_K, "rk"), (TO_S0, "s0b"), (TO_W0, "w0b"), (BACK_0, "r0")):
        wide_sent(kind, buf[name])


def section_kernel(wave, slope, out):
    out[...] = wave[...] + half_step * slope[...]


def result_kernel(wave, h0, y1, base1, slope, following):
    first = y1[...] + base1[...]
    second = -h0[...]
    slope[0] = first
    slope[1] = second
    following[0] = wave[0] + half_step * first
    following[1] = wave[1] + half_step * second


def local(wide, wavefunction, previous_slope, potential, kinetic_one, coupling_one, kinetic_two, coupling_two, kinetic_three, coupling_three):
    _, rows, second, third = wavefunction.shape
    full = rows * wide
    q = second // wide
    own = jnp.stack([kinetic_two, coupling_two])
    ends = lax.ppermute(own, "narrow", [(0, 1), (3, 2)])
    w = jnp.concatenate([own[0], ends[0], own[1], ends[1]], axis=0)
    wt = w.T

    block = 8
    pair = pl.BlockSpec((2, block, second, third), lambda i: (0, i, 0, 0))
    section = pl.pallas_call(
        section_kernel, grid=(rows // block,), in_specs=[pair, pair], out_specs=pair,
        out_shape=jax.ShapeDtypeStruct(wavefunction.shape, jnp.float32),
        compiler_params=pltpu.CompilerParams(vmem_limit_bytes=40 * 2**20),
        cost_estimate=pl.CostEstimate(flops=wavefunction.size * 2, bytes_accessed=wavefunction.size * 12, transcendentals=0),
    )(wavefunction, previous_slope)

    shapes = []
    for name in BUFFERS:
        if name in WIDE_SHAPED:
            shape = (q, full, third)
        elif name in SECOND_FIRST:
            shape = (second, rows, third)
        else:
            shape = (rows, second, third)
        shapes.append(jax.ShapeDtypeStruct(shape, jnp.float32))
    nc = rows // 8
    bf = jnp.bfloat16
    everything = 4 * second
    outs = pl.pallas_call(
        functools.partial(kernel, wide),
        out_shape=shapes,
        in_specs=[pl.BlockSpec(memory_space=pl.ANY)] * 2 + [pl.BlockSpec(memory_space=pltpu.VMEM)] * 6,
        out_specs=[pl.BlockSpec(memory_space=pl.ANY)] * len(BUFFERS),
        scratch_shapes=[pltpu.VMEM((everything, everything), bf)] * 4
        + [pltpu.VMEM((full, full), bf)] * 4
        + [pltpu.VMEM((third, third), bf)] * 4
        + [
            pltpu.VMEM((everything, third), bf),
            pltpu.VMEM((everything, third), bf),
            pltpu.VMEM((4, second, third), jnp.float32),
            pltpu.SemaphoreType.DMA((10, nc)),
            pltpu.SemaphoreType.DMA((10, nc)),
            pltpu.SemaphoreType.DMA((6,)),
            pltpu.SemaphoreType.DMA((6,)),
            pltpu.SemaphoreType.DMA((6,)),
        ],
        compiler_params=pltpu.CompilerParams(collective_id=0, has_side_effects=True, vmem_limit_bytes=52 * 2**20),
        cost_estimate=pl.CostEstimate(flops=6 * 3584 * 2 * rows * second * third * 2, bytes_accessed=40 * rows * second * third * 4, transcendentals=0),
    )(section, potential, w, wt, kinetic_one, coupling_one, kinetic_three, coupling_three)
    buf = dict(zip(BUFFERS, outs))

    one = pl.BlockSpec((block, second, third), lambda i: (i, 0, 0))
    return pl.pallas_call(
        result_kernel, grid=(rows // block,), in_specs=[pair, one, one, one], out_specs=[pair, pair],
        out_shape=[jax.ShapeDtypeStruct(wavefunction.shape, jnp.float32)] * 2,
        compiler_params=pltpu.CompilerParams(vmem_limit_bytes=40 * 2**20),
        cost_estimate=pl.CostEstimate(flops=wavefunction.size * 3, bytes_accessed=wavefunction.size * 18, transcendentals=0),
    )(wavefunction, buf["h0"], buf["y1"], buf["base1"])


def solution(mesh):
    wide = mesh.shape["wide"]
    field = P(None, "wide", "narrow", None)
    in_specs = (field, field, P("wide", "narrow", None), P(), P(), P("narrow", None), P("narrow", None), P(), P())

    def body(*arrays):
        return tuple(local(wide, *arrays))

    def run(*arrays):
        with jax.sharding.use_abstract_mesh(mesh.abstract_mesh):
            return jax.shard_map(body, mesh=mesh, in_specs=in_specs, out_specs=(field, field), check_vma=False)(*arrays)

    return run
```

```python
import functools

import jax
import jax.numpy as jnp
from jax import lax
from jax.experimental import pallas as pl
from jax.experimental.pallas import tpu as pltpu
from jax.sharding import PartitionSpec as P

half_step = 0.1
MESH = pl.DeviceIdType.MESH
OWN, END, FWD, YROW, WROW, PSI, PHI, SUM_O, SUM_F, YEND = range(10)
TO_S1, BACK_C, BACK_K, TO_S0, TO_W0, BACK_0 = range(6)
BUFFERS = (
    "end0", "other0", "far0", "y0", "w0", "sy", "sw",
    "s0b", "t0", "w0b", "tw", "r0", "b0",
    "s1b", "t1", "rc", "rk", "bc", "bk", "phi",
    "psie", "phie", "po", "pe", "ao", "af", "ba0", "ba1", "se", "y1", "s0", "s1",
)
WIDE_SHAPED = ("t0", "tw", "r0", "t1", "rc", "rk")
SECOND_FIRST = ("s0b", "w0b", "b0", "s1b", "bc", "bk")


def halves(x):
    high = x.astype(jnp.bfloat16)
    return high, (x - high.astype(jnp.float32)).astype(jnp.bfloat16)


def dot3(ah, al, bh, bl):
    dot = functools.partial(jnp.dot, preferred_element_type=jnp.float32)
    return dot(ah, bh) + dot(ah, bl) + dot(al, bh)


def kernel(wide, wave, prev, pot, k2, c2, k1, c1, k3, c3, *refs):
    buf = dict(zip(BUFFERS, refs[:len(BUFFERS)]))
    (results, wh, wl, wth, wtl, k1h, k1l, c1h, c1l, k3h, k3l, c3h, c3l, fh, fl, gather, wend,
     zs, zr, es, er, ws, wr, wloc) = refs[len(BUFFERS):]
    rows, second, third = wave.shape[1:]
    full = rows * wide
    q = second // wide
    step = 8
    nc = rows // step
    me = lax.axis_index("wide")
    z = lax.axis_index("narrow")
    hub = jnp.logical_or(z == 1, z == 2)
    end = jnp.where(z == 1, 0, 3)
    other = 3 - z
    far = 3 - end
    my_hub = jnp.where(z == 0, 1, 2)
    slope, following = results.at[pl.ds(0, 2)], results.at[pl.ds(2, 2)]
    s0, s1 = buf["s0"], buf["s1"]

    def peer_of(d):
        return lax.rem(me + d, wide)

    barrier = pltpu.get_barrier_semaphore()

    def greet(d, carry):
        pl.semaphore_signal(barrier, inc=1, device_id={"wide": peer_of(d)}, device_id_type=MESH)
        return carry

    lax.fori_loop(1, wide, greet, 0)

    @pl.when(hub)
    def _():
        pl.semaphore_signal(barrier, inc=1, device_id={"narrow": end}, device_id_type=MESH)
        pl.semaphore_signal(barrier, inc=1, device_id={"narrow": other}, device_id_type=MESH)

    @pl.when(jnp.logical_not(hub))
    def _():
        pl.semaphore_signal(barrier, inc=1, device_id={"narrow": my_hub}, device_id_type=MESH)

    def piece(ref, c):
        return ref.at[pl.ds(pl.multiple_of(c * step, step), step)]

    def zcopy(kind, c, src, dst, target):
        return pltpu.make_async_remote_copy(
            src_ref=piece(src, c), dst_ref=piece(dst, c), send_sem=zs.at[kind, c], recv_sem=zr.at[kind, c],
            device_id={"narrow": target}, device_id_type=MESH)

    def zrecv(kind, c, dst):
        pltpu.make_async_copy(piece(dst, c), piece(dst, c), zr.at[kind, c]).wait()

    def zsent(kind, c, src):
        pltpu.make_async_copy(piece(src, c), piece(src, c), zs.at[kind, c]).wait()

    def end_matrix(n, matrix):
        return pltpu.make_async_remote_copy(
            src_ref=matrix, dst_ref=wend.at[n], send_sem=es.at[n], recv_sem=er.at[n],
            device_id={"narrow": my_hub}, device_id_type=MESH)

    def each_chunk(f):
        def body(c, carry):
            f(c)
            return carry
        lax.fori_loop(0, nc, body, 0)

    def mine_of(ref, index, size):
        return ref.at[:, pl.ds(pl.multiple_of(index * size, size), size)]

    def to_whole(kind, src, dst):
        def send(d, carry):
            p = peer_of(d)
            pltpu.make_async_remote_copy(
                src_ref=src.at[pl.ds(p * q, q)], dst_ref=mine_of(dst, me, rows),
                send_sem=ws.at[kind], recv_sem=wr.at[kind], device_id={"wide": p}, device_id_type=MESH).start()
            return carry
        lax.fori_loop(1, wide, send, 0)
        pltpu.make_async_copy(src.at[pl.ds(me * q, q)], mine_of(dst, me, rows), wloc.at[kind]).start()

    def to_whole_wait(kind, dst):
        part = dst.at[:, pl.ds(0, (wide - 1) * rows)]
        pltpu.make_async_copy(part, part, wr.at[kind]).wait()
        own = dst.at[:, pl.ds(0, rows)]
        pltpu.make_async_copy(own, own, wloc.at[kind]).wait()

    def from_whole(kind, src, dst):
        def send(d, carry):
            p = peer_of(d)
            pltpu.make_async_remote_copy(
                src_ref=mine_of(src, p, rows), dst_ref=dst.at[pl.ds(me * q, q)],
                send_sem=ws.at[kind], recv_sem=wr.at[kind], device_id={"wide": p}, device_id_type=MESH).start()
            return carry
        lax.fori_loop(1, wide, send, 0)
        pltpu.make_async_copy(mine_of(src, me, rows), dst.at[pl.ds(me * q, q)], wloc.at[kind]).start()

    def from_whole_wait(kind, dst):
        part = dst.at[pl.ds(0, (wide - 1) * q)]
        pltpu.make_async_copy(part, part, wr.at[kind]).wait()
        own = dst.at[pl.ds(0, q)]
        pltpu.make_async_copy(own, own, wloc.at[kind]).wait()

    def wide_sent(kind, src):
        part = src.at[pl.ds(0, (wide - 1) * q)] if src.shape[0] == second else src.at[:, pl.ds(0, (wide - 1) * rows)]
        pltpu.make_async_copy(part, part, ws.at[kind]).wait()

    by_first = pl.BlockSpec((step, second, third), lambda i: (i, 0, 0))
    by_second = pl.BlockSpec((second, step, third), lambda i: (0, i, 0))
    one_row = pl.BlockSpec((1, second, third), lambda i: (i, 0, 0))
    one_whole = pl.BlockSpec((1, full, third), lambda i: (i, 0, 0))

    parts = 2
    half_first = pl.BlockSpec((step, second // parts, third), lambda i, j: (i, j, 0))
    half_second = pl.BlockSpec((second // parts, step, third), lambda i, j: (j, i, 0))
    quarter = pl.BlockSpec((step // 2, second, third), lambda i: (i, 0, 0))

    def transpose_stage(src, dst):
        def body(x, out):
            for g in range(second // 8):
                out[8 * g:8 * g + 8, :, :] = jnp.swapaxes(x[:, 8 * g:8 * g + 8, :], 0, 1)
        pltpu.emit_pipeline(body, grid=(nc,), in_specs=[by_first], out_specs=[by_second])(src, dst)

    def section_stage(start, size):
        def body(x, y, out):
            out[...] = x[...] + half_step * y[...]
        cut = pl.ds(start, size)
        pltpu.emit_pipeline(body, grid=(size * 2 // step,), in_specs=[quarter] * 2, out_specs=[quarter])(
            wave.at[0, cut], prev.at[0, cut], s0.at[cut])

    def section_swapped_stage():
        def body(x, y, out, out_swapped):
            for g in range(second // 8):
                cut = slice(8 * g, 8 * g + 8)
                value = x[:, cut, :] + half_step * y[:, cut, :]
                out[:, cut, :] = value
                out_swapped[cut, :, :] = jnp.swapaxes(value, 0, 1)
        pltpu.emit_pipeline(body, grid=(nc,), in_specs=[by_first] * 2, out_specs=[by_first, by_second])(
            wave.at[1], prev.at[1], s1, buf["s1b"])

    def third_dot(x, mh, ml):
        xh, xl = halves(x)
        return dot3(xh, xl, mh[...], ml[...])

    group = 32

    def phi_stage(src, dst):
        def body(x, out):
            for g in range(second // group):
                block = x[group * g:group * (g + 1)].reshape(group * step, third)
                result = third_dot(block, c3h, c3l).reshape(group, step, third)
                out[:, group * g:group * (g + 1), :] = jnp.swapaxes(result, 0, 1)
        pltpu.emit_pipeline(body, grid=(nc,), in_specs=[by_second], out_specs=[by_first])(src, dst)

    def coupled_stage(src, dst):
        def body(x, out):
            for g in range(second // group):
                block = x[:, group * g:group * (g + 1), :].reshape(group * step, third)
                result = third_dot(block, c3h, c3l).reshape(step, group, third)
                out[group * g:group * (g + 1), :, :] = jnp.swapaxes(result, 0, 1)
        pltpu.emit_pipeline(body, grid=(nc,), in_specs=[by_first], out_specs=[by_second])(src, dst)

    def base_stage(field, returned, start, sign, slot, extra=None):
        def body(x, v, back, base, *rest):
            out, out_next = rest[-2:]
            for g in range(second // parts // group):
                cut = slice(group * g, group * (g + 1))
                block = x[:, cut, :].reshape(group * step, third)
                result = third_dot(block, k3h, k3l).reshape(step, group, third)
                result = result + v[:, cut, :] * x[:, cut, :] + jnp.swapaxes(back[cut], 0, 1)
                if extra is not None:
                    result = result + rest[0][:, cut, :]
                result = sign * result
                out[:, cut, :] = result
                out_next[:, cut, :] = base[:, cut, :] + half_step * result
        ins = [field, pot, returned, start] + ([] if extra is None else [extra])
        specs = [half_first, half_first, half_second, half_first] + ([] if extra is None else [half_first])
        pltpu.emit_pipeline(body, grid=(nc, parts), in_specs=specs, out_specs=[half_first] * 2)(
            *ins, slope.at[slot], following.at[slot])

    def first_stage(terms, dst):
        def body(*args):
            out = args[-1]
            total = None
            for (_, mh, ml), x in zip(terms, args[:-1]):
                xh, xl = halves(x[0])
                value = dot3(mh[...], ml[...], xh, xl)
                total = value if total is None else total + value
            out[0] = total
        pltpu.emit_pipeline(body, grid=(q,), in_specs=[one_whole] * len(terms), out_specs=[one_whole])(
            *[t[0] for t in terms], dst)

    def place(slot, x):
        at = pl.ds(pl.multiple_of(slot * second, second), second)
        high, low = halves(x)
        fh[at, :] = high
        fl[at, :] = low

    def gather_stage(c):
        def body(own, e, o, f, y, v, ye, ve):
            place(z, own[0])
            place(end, e[0])
            place(other, o[0])
            place(far, f[0])
            for n, out in enumerate((y, ye, v, ve)):
                cut = slice(n * second, (n + 1) * second)
                out[0] = dot3(wh[cut, :], wl[cut, :], fh[...], fl[...])
        pltpu.emit_pipeline(body, grid=(step,), in_specs=[one_row] * 4, out_specs=[one_row] * 4)(
            piece(s0, c), piece(buf["end0"], c), piece(buf["other0"], c), piece(buf["far0"], c),
            piece(buf["y0"], c), piece(buf["w0"], c), piece(buf["sy"], c), piece(buf["sw"], c))

    def scatter_stage(c):
        def body(own, e, pown, pend, yo, ye, ao, af):
            place(0, own[0])
            place(1, e[0])
            place(2, pown[0])
            place(3, pend[0])
            for n in range(4):
                cut = slice(n * second, (n + 1) * second)
                gather[n] = dot3(wth[cut, :], wtl[cut, :], fh[...], fl[...])
            yo[0] = gather[z]
            ye[0] = gather[end]
            ao[0] = gather[other]
            af[0] = gather[far]
        pltpu.emit_pipeline(body, grid=(step,), in_specs=[one_row] * 4, out_specs=[one_row] * 4)(
            piece(s1, c), piece(buf["psie"], c), piece(buf["phi"], c), piece(buf["phie"], c),
            piece(buf["po"], c), piece(buf["pe"], c), piece(buf["ao"], c), piece(buf["af"], c))

    def end_sum_stage(c):
        def body(x, y, out):
            out[...] = x[...] + y[...]
        pltpu.emit_pipeline(body, grid=(2,), in_specs=[quarter] * 2, out_specs=[quarter])(
            piece(buf["pe"], c), piece(buf["ba1"], c), piece(buf["se"], c))

    def own_sum_stage(c, *terms):
        def body(*args):
            value = args[0][...]
            for term in args[1:-2]:
                value = value + term[...]
            args[-2][...] += value
            args[-1][...] += half_step * value
        pltpu.emit_pipeline(body, grid=(2,), in_specs=[quarter] * len(terms), out_specs=[quarter] * 2)(
            *[piece(buf[term], c) for term in terms], piece(slope.at[0], c), piece(following.at[0], c))

    ahead = min(3, nc)
    section_stage(0, step)

    @pl.when(hub)
    def _():
        pl.semaphore_wait(barrier, wide + 1)
        zcopy(OWN, 0, s0, buf["other0"], other).start()

    @pl.when(jnp.logical_not(hub))
    def _():
        pl.semaphore_wait(barrier, wide)
        zcopy(END, 0, s0, buf["end0"], my_hub).start()
        for n, matrix in enumerate((k2, c2)):
            end_matrix(n, matrix).start()

    if nc > 1:
        section_stage(step, rows - step)

        @pl.when(hub)
        def _():
            for c in range(1, ahead):
                zcopy(OWN, c, s0, buf["other0"], other).start()

        @pl.when(jnp.logical_not(hub))
        def _():
            for c in range(1, nc):
                zcopy(END, c, s0, buf["end0"], my_hub).start()

    section_swapped_stage()
    to_whole(TO_S1, buf["s1b"], buf["t1"])
    for matrix, high, low in ((c1, c1h, c1l), (c3, c3h, c3l), (k1, k1h, k1l), (k3, k3h, k3l)):
        high[...], low[...] = halves(matrix[...])

    @pl.when(hub)
    def _():
        for n, matrix in enumerate((k2, c2)):
            end_matrix(n, matrix).wait_recv()
            for m, rows_of in enumerate((matrix, wend.at[n])):
                cut = slice((2 * n + m) * second, (2 * n + m + 1) * second)
                value = rows_of[...]
                wh[cut, :], wl[cut, :] = halves(value)
                wth[:, cut], wtl[:, cut] = halves(value.T)

    first_at = min(3, nc - 1)
    phi_at = min(5, nc - 1)
    base_at = nc
    coupled_at = nc + 1
    second_at = min(nc + 4, 2 * nc)
    last_at = max(2 * nc - 1, second_at)
    early = nc // 2

    def body(t, carry):
        @pl.when(jnp.logical_and(hub, t + ahead < nc))
        def _():
            zcopy(OWN, t + ahead, s0, buf["other0"], other).start()

        @pl.when(jnp.logical_and(hub, t < nc))
        def _():
            zrecv(END, t, buf["end0"])
            zcopy(FWD, t, buf["end0"], buf["far0"], other).start()

        @pl.when(t == first_at)
        def _():
            to_whole_wait(TO_S1, buf["t1"])
            first_stage([(buf["t1"], c1h, c1l)], buf["rc"])
            from_whole(BACK_C, buf["rc"], buf["bc"])

            @pl.when(jnp.logical_not(hub))
            def _():
                for c in range(early):
                    zcopy(PSI, c, s1, buf["psie"], my_hub).start()
            first_stage([(buf["t1"], k1h, k1l)], buf["rk"])
            transpose_stage(s0, buf["s0b"])

        @pl.when(t == phi_at)
        def _():
            from_whole_wait(BACK_C, buf["bc"])
            phi_stage(buf["bc"], buf["phi"])

            @pl.when(jnp.logical_not(hub))
            def _():
                for c in range(nc):
                    if c >= early:
                        zcopy(PSI, c, s1, buf["psie"], my_hub).start()
                    zcopy(PHI, c, buf["phi"], buf["phie"], my_hub).start()
            from_whole(BACK_K, buf["rk"], buf["bk"])
            to_whole(TO_S0, buf["s0b"], buf["t0"])

        @pl.when(jnp.logical_and(hub, jnp.logical_and(t >= nc - 1, t <= 2 * nc - 2)))
        def _():
            c = t - (nc - 1)
            zrecv(PSI, c, buf["psie"])
            zrecv(PHI, c, buf["phie"])
            scatter_stage(c)
            zcopy(SUM_F, c, buf["af"], buf["ba1"], other).start()
            zcopy(SUM_O, c, buf["ao"], buf["ba0"], other).start()

        @pl.when(jnp.logical_and(hub, jnp.logical_and(t >= 1, t <= nc)))
        def _():
            c = t - 1
            zrecv(OWN, c, buf["other0"])
            zrecv(FWD, c, buf["far0"])
            gather_stage(c)
            zcopy(WROW, c, buf["sw"], buf["w0"], end).start()
            zcopy(YROW, c, buf["sy"], buf["y0"], end).start()

        @pl.when(jnp.logical_and(hub, t >= nc + 1))
        def _():
            c = t - (nc + 1)
            zrecv(SUM_F, c, buf["ba1"])
            end_sum_stage(c)
            zcopy(YEND, c, buf["se"], buf["y1"], end).start()
            zrecv(SUM_O, c, buf["ba0"])
            own_sum_stage(c, "po", "ba0")

        @pl.when(t == base_at)
        def _():
            from_whole_wait(BACK_K, buf["bk"])
            base_stage(s1, buf["bk"], wave.at[0], 1.0, 0)

        @pl.when(t == coupled_at)
        def _():
            @pl.when(jnp.logical_not(hub))
            def _():
                each_chunk(lambda c: zrecv(WROW, c, buf["w0"]))
            coupled_stage(buf["w0"], buf["w0b"])
            to_whole(TO_W0, buf["w0b"], buf["tw"])

        @pl.when(t == second_at)
        def _():
            to_whole_wait(TO_S0, buf["t0"])
            to_whole_wait(TO_W0, buf["tw"])
            first_stage([(buf["t0"], k1h, k1l), (buf["tw"], c1h, c1l)], buf["r0"])
            from_whole(BACK_0, buf["r0"], buf["b0"])

        @pl.when(t == last_at)
        def _():
            @pl.when(jnp.logical_not(hub))
            def _():
                each_chunk(lambda c: zrecv(YROW, c, buf["y0"]))
            from_whole_wait(BACK_0, buf["b0"])
            base_stage(s0, buf["b0"], wave.at[1], -1.0, 1, buf["y0"])
        return carry

    lax.fori_loop(0, 2 * nc + 1, body, 0)

    @pl.when(hub)
    def _():
        def sent(c):
            for kind, name in ((OWN, "s0"), (FWD, "end0"), (YROW, "sy"), (WROW, "sw"), (SUM_O, "ao"), (SUM_F, "af"), (YEND, "se")):
                zsent(kind, c, buf[name])
        each_chunk(sent)

    @pl.when(jnp.logical_not(hub))
    def _():
        def sent(c):
            zsent(END, c, s0)
            zsent(PSI, c, s1)
            zsent(PHI, c, buf["phi"])
            zrecv(YEND, c, buf["y1"])
            own_sum_stage(c, "y1")
        each_chunk(sent)
        for n, matrix in enumerate((k2, c2)):
            end_matrix(n, matrix).wait_send()

    for kind, name in ((TO_S1, "s1b"), (BACK_C, "rc"), (BACK_K, "rk"), (TO_S0, "s0b"), (TO_W0, "w0b"), (BACK_0, "r0")):
        wide_sent(kind, buf[name])


def write_kernel(results, slope_out, following_out, sems):
    copies = [
        pltpu.make_async_copy(results.at[pl.ds(0, 2)], slope_out, sems.at[0]),
        pltpu.make_async_copy(results.at[pl.ds(2, 2)], following_out, sems.at[1]),
    ]
    for copy in copies:
        copy.start()
    for copy in copies:
        copy.wait()


def local(wide, wavefunction, previous_slope, potential, kinetic_one, coupling_one, kinetic_two, coupling_two, kinetic_three, coupling_three):
    _, rows, second, third = wavefunction.shape
    full = rows * wide
    q = second // wide
    shapes = []
    for name in BUFFERS:
        if name in WIDE_SHAPED:
            shape = (q, full, third)
        elif name in SECOND_FIRST:
            shape = (second, rows, third)
        else:
            shape = (rows, second, third)
        shapes.append(jax.ShapeDtypeStruct(shape, jnp.float32))
    shapes += [pltpu.VMEM((4, rows, second, third), jnp.float32)]
    nc = rows // 8
    bf = jnp.bfloat16
    everything = 4 * second
    outs = pl.pallas_call(
        functools.partial(kernel, wide),
        out_shape=shapes,
        in_specs=[pl.BlockSpec(memory_space=pl.ANY)] * 3 + [pl.BlockSpec(memory_space=pltpu.VMEM)] * 6,
        out_specs=[pl.BlockSpec(memory_space=pl.ANY)] * len(BUFFERS) + [pl.BlockSpec(memory_space=pltpu.VMEM)],
        scratch_shapes=[pltpu.VMEM((everything, everything), bf)] * 4
        + [pltpu.VMEM((full, full), bf)] * 4
        + [pltpu.VMEM((third, third), bf)] * 4
        + [
            pltpu.VMEM((everything, third), bf),
            pltpu.VMEM((everything, third), bf),
            pltpu.VMEM((4, second, third), jnp.float32),
            pltpu.VMEM((2, second, everything), jnp.float32),
            pltpu.SemaphoreType.DMA((10, nc)),
            pltpu.SemaphoreType.DMA((10, nc)),
            pltpu.SemaphoreType.DMA((2,)),
            pltpu.SemaphoreType.DMA((2,)),
            pltpu.SemaphoreType.DMA((6,)),
            pltpu.SemaphoreType.DMA((6,)),
            pltpu.SemaphoreType.DMA((6,)),
        ],
        compiler_params=pltpu.CompilerParams(collective_id=0, has_side_effects=True, vmem_limit_bytes=26 * 2**20),
        cost_estimate=pl.CostEstimate(flops=6 * 3584 * 2 * rows * second * third * 2, bytes_accessed=40 * rows * second * third * 4, transcendentals=0),
    )(wavefunction, previous_slope, potential, kinetic_two, coupling_two, kinetic_one, coupling_one, kinetic_three, coupling_three)
    return pl.pallas_call(
        write_kernel,
        in_specs=[pl.BlockSpec(memory_space=pltpu.VMEM)],
        out_specs=[pl.BlockSpec(memory_space=pl.ANY)] * 2,
        out_shape=[jax.ShapeDtypeStruct(wavefunction.shape, jnp.float32)] * 2,
        scratch_shapes=[pltpu.SemaphoreType.DMA((2,))],
        compiler_params=pltpu.CompilerParams(vmem_limit_bytes=2**20),
        cost_estimate=pl.CostEstimate(flops=0, bytes_accessed=wavefunction.size * 8, transcendentals=0),
    )(*outs[len(BUFFERS):])


def solution(mesh):
    wide = mesh.shape["wide"]
    field = P(None, "wide", "narrow", None)
    in_specs = (field, field, P("wide", "narrow", None), P(), P(), P("narrow", None), P("narrow", None), P(), P())

    def body(*arrays):
        return tuple(local(wide, *arrays))

    def run(*arrays):
        with jax.sharding.use_abstract_mesh(mesh.abstract_mesh):
            return jax.shard_map(body, mesh=mesh, in_specs=in_specs, out_specs=(field, field), check_vma=False)(*arrays)

    return run
```

```python
import functools

import jax
import jax.numpy as jnp
from jax import lax
from jax.experimental import pallas as pl
from jax.experimental.pallas import tpu as pltpu
from jax.sharding import PartitionSpec as P

half_step = 0.1
MESH = pl.DeviceIdType.MESH
OWN, END, FWD, YROW, WROW, PSI, PHI, SUM_O, SUM_F, YEND = range(10)
TO_S1, BACK_C, BACK_K, TO_S0, TO_W0, BACK_0 = range(6)
BUFFERS = (
    "end0", "other0", "far0", "y0", "w0", "sy", "sw",
    "s0b", "t0", "w0b", "tw", "r0", "b0",
    "s1b", "t1", "rc", "rk", "bc", "bk", "phi",
    "psie", "phie", "po", "pe", "ao", "af", "ba0", "ba1", "se", "y1", "s0", "s1",
)
WIDE_SHAPED = ("t0", "tw", "r0", "t1", "rc", "rk")
SECOND_FIRST = ("s0b", "w0b", "b0", "s1b", "bc", "bk")


def halves(x):
    high = x.astype(jnp.bfloat16)
    return high, (x - high.astype(jnp.float32)).astype(jnp.bfloat16)


def dot3(ah, al, bh, bl):
    dot = functools.partial(jnp.dot, preferred_element_type=jnp.float32)
    return dot(ah, bh) + dot(ah, bl) + dot(al, bh)


def kernel(wide, wave, prev, pot, k2, c2, k1, c1, k3, c3, *refs):
    buf = dict(zip(BUFFERS, refs[:len(BUFFERS)]))
    (results, wh, wl, wth, wtl, k1h, k1l, c1h, c1l, k3h, k3l, c3h, c3l, fh, fl, gather, wend,
     k2v, c2v, k1v, c1v, k3v, c3v, zs, zr, es, er, ms, ws, wr, wloc) = refs[len(BUFFERS):]
    rows, second, third = wave.shape[1:]
    full = rows * wide
    q = second // wide
    step = 8
    nc = rows // step
    me = lax.axis_index("wide")
    z = lax.axis_index("narrow")
    hub = jnp.logical_or(z == 1, z == 2)
    end = jnp.where(z == 1, 0, 3)
    other = 3 - z
    far = 3 - end
    my_hub = jnp.where(z == 0, 1, 2)
    slope, following = results.at[pl.ds(0, 2)], results.at[pl.ds(2, 2)]
    s0, s1 = buf["s0"], buf["s1"]

    def peer_of(d):
        return lax.rem(me + d, wide)

    barrier = pltpu.get_barrier_semaphore()

    def greet(d, carry):
        pl.semaphore_signal(barrier, inc=1, device_id={"wide": peer_of(d)}, device_id_type=MESH)
        return carry

    lax.fori_loop(1, wide, greet, 0)

    @pl.when(hub)
    def _():
        pl.semaphore_signal(barrier, inc=1, device_id={"narrow": end}, device_id_type=MESH)
        pl.semaphore_signal(barrier, inc=1, device_id={"narrow": other}, device_id_type=MESH)

    @pl.when(jnp.logical_not(hub))
    def _():
        pl.semaphore_signal(barrier, inc=1, device_id={"narrow": my_hub}, device_id_type=MESH)

    def piece(ref, c):
        return ref.at[pl.ds(pl.multiple_of(c * step, step), step)]

    def zcopy(kind, c, src, dst, target):
        return pltpu.make_async_remote_copy(
            src_ref=piece(src, c), dst_ref=piece(dst, c), send_sem=zs.at[kind, c], recv_sem=zr.at[kind, c],
            device_id={"narrow": target}, device_id_type=MESH)

    def zrecv(kind, c, dst):
        pltpu.make_async_copy(piece(dst, c), piece(dst, c), zr.at[kind, c]).wait()

    def zsent(kind, c, src):
        pltpu.make_async_copy(piece(src, c), piece(src, c), zs.at[kind, c]).wait()

    def end_matrix(n, matrix):
        return pltpu.make_async_remote_copy(
            src_ref=matrix, dst_ref=wend.at[n], send_sem=es.at[n], recv_sem=er.at[n],
            device_id={"narrow": my_hub}, device_id_type=MESH)

    def each_chunk(f):
        def body(c, carry):
            f(c)
            return carry
        lax.fori_loop(0, nc, body, 0)

    def mine_of(ref, index, size):
        return ref.at[:, pl.ds(pl.multiple_of(index * size, size), size)]

    def to_whole(kind, src, dst):
        def send(d, carry):
            p = peer_of(d)
            pltpu.make_async_remote_copy(
                src_ref=src.at[pl.ds(p * q, q)], dst_ref=mine_of(dst, me, rows),
                send_sem=ws.at[kind], recv_sem=wr.at[kind], device_id={"wide": p}, device_id_type=MESH).start()
            return carry
        lax.fori_loop(1, wide, send, 0)
        pltpu.make_async_copy(src.at[pl.ds(me * q, q)], mine_of(dst, me, rows), wloc.at[kind]).start()

    def to_whole_wait(kind, dst):
        part = dst.at[:, pl.ds(0, (wide - 1) * rows)]
        pltpu.make_async_copy(part, part, wr.at[kind]).wait()
        own = dst.at[:, pl.ds(0, rows)]
        pltpu.make_async_copy(own, own, wloc.at[kind]).wait()

    def from_whole(kind, src, dst):
        def send(d, carry):
            p = peer_of(d)
            pltpu.make_async_remote_copy(
                src_ref=mine_of(src, p, rows), dst_ref=dst.at[pl.ds(me * q, q)],
                send_sem=ws.at[kind], recv_sem=wr.at[kind], device_id={"wide": p}, device_id_type=MESH).start()
            return carry
        lax.fori_loop(1, wide, send, 0)
        pltpu.make_async_copy(mine_of(src, me, rows), dst.at[pl.ds(me * q, q)], wloc.at[kind]).start()

    def from_whole_wait(kind, dst):
        part = dst.at[pl.ds(0, (wide - 1) * q)]
        pltpu.make_async_copy(part, part, wr.at[kind]).wait()
        own = dst.at[pl.ds(0, q)]
        pltpu.make_async_copy(own, own, wloc.at[kind]).wait()

    def wide_sent(kind, src):
        part = src.at[pl.ds(0, (wide - 1) * q)] if src.shape[0] == second else src.at[:, pl.ds(0, (wide - 1) * rows)]
        pltpu.make_async_copy(part, part, ws.at[kind]).wait()

    by_first = pl.BlockSpec((step, second, third), lambda i: (i, 0, 0))
    by_second = pl.BlockSpec((second, step, third), lambda i: (0, i, 0))
    one_row = pl.BlockSpec((1, second, third), lambda i: (i, 0, 0))
    one_whole = pl.BlockSpec((1, full, third), lambda i: (i, 0, 0))

    parts = 2
    half_first = pl.BlockSpec((step, second // parts, third), lambda i, j: (i, j, 0))
    half_second = pl.BlockSpec((second // parts, step, third), lambda i, j: (j, i, 0))
    quarter = pl.BlockSpec((step // 2, second, third), lambda i: (i, 0, 0))

    def transpose_stage(src, dst):
        def body(x, out):
            for g in range(second // 8):
                out[8 * g:8 * g + 8, :, :] = jnp.swapaxes(x[:, 8 * g:8 * g + 8, :], 0, 1)
        pltpu.emit_pipeline(body, grid=(nc,), in_specs=[by_first], out_specs=[by_second])(src, dst)

    def section_stage(start, size, block):
        spec = pl.BlockSpec((block, second, third), lambda i: (i, 0, 0))

        def body(x, y, out):
            out[...] = x[...] + half_step * y[...]
        cut = pl.ds(start, size)
        pltpu.emit_pipeline(body, grid=(size // block,), in_specs=[spec] * 2, out_specs=[spec])(
            wave.at[0, cut], prev.at[0, cut], s0.at[cut])

    def section_swapped_stage():
        def body(x, y, out, out_swapped):
            for g in range(second // 8):
                cut = slice(8 * g, 8 * g + 8)
                value = x[:, cut, :] + half_step * y[:, cut, :]
                out[:, cut, :] = value
                out_swapped[cut, :, :] = jnp.swapaxes(value, 0, 1)
        pltpu.emit_pipeline(body, grid=(nc,), in_specs=[by_first] * 2, out_specs=[by_first, by_second])(
            wave.at[1], prev.at[1], s1, buf["s1b"])

    def third_dot(x, mh, ml):
        xh, xl = halves(x)
        return dot3(xh, xl, mh[...], ml[...])

    group = 32

    def phi_stage(src, dst):
        def body(x, out):
            for g in range(second // group):
                block = x[group * g:group * (g + 1)].reshape(group * step, third)
                result = third_dot(block, c3h, c3l).reshape(group, step, third)
                out[:, group * g:group * (g + 1), :] = jnp.swapaxes(result, 0, 1)
        pltpu.emit_pipeline(body, grid=(nc,), in_specs=[by_second], out_specs=[by_first])(src, dst)

    def coupled_stage(src, dst):
        def body(x, out):
            for g in range(second // group):
                block = x[:, group * g:group * (g + 1), :].reshape(group * step, third)
                result = third_dot(block, c3h, c3l).reshape(step, group, third)
                out[group * g:group * (g + 1), :, :] = jnp.swapaxes(result, 0, 1)
        pltpu.emit_pipeline(body, grid=(nc,), in_specs=[by_first], out_specs=[by_second])(src, dst)

    def base_stage(field, returned, start, sign, slot, extra=None):
        def body(x, v, back, base, *rest):
            out, out_next = rest[-2:]
            for g in range(second // parts // group):
                cut = slice(group * g, group * (g + 1))
                block = x[:, cut, :].reshape(group * step, third)
                result = third_dot(block, k3h, k3l).reshape(step, group, third)
                result = result + v[:, cut, :] * x[:, cut, :] + jnp.swapaxes(back[cut], 0, 1)
                if extra is not None:
                    result = result + rest[0][:, cut, :]
                result = sign * result
                out[:, cut, :] = result
                out_next[:, cut, :] = base[:, cut, :] + half_step * result
        ins = [field, pot, returned, start] + ([] if extra is None else [extra])
        specs = [half_first, half_first, half_second, half_first] + ([] if extra is None else [half_first])
        pltpu.emit_pipeline(body, grid=(nc, parts), in_specs=specs, out_specs=[half_first] * 2)(
            *ins, slope.at[slot], following.at[slot])

    def first_stage(terms, dst):
        def body(*args):
            out = args[-1]
            total = None
            for (_, mh, ml), x in zip(terms, args[:-1]):
                xh, xl = halves(x[0])
                value = dot3(mh[...], ml[...], xh, xl)
                total = value if total is None else total + value
            out[0] = total
        pltpu.emit_pipeline(body, grid=(q,), in_specs=[one_whole] * len(terms), out_specs=[one_whole])(
            *[t[0] for t in terms], dst)

    def place(slot, x):
        at = pl.ds(pl.multiple_of(slot * second, second), second)
        high, low = halves(x)
        fh[at, :] = high
        fl[at, :] = low

    def gather_stage(c):
        def body(own, e, o, f, y, v, ye, ve):
            place(z, own[0])
            place(end, e[0])
            place(other, o[0])
            place(far, f[0])
            for n, out in enumerate((y, ye, v, ve)):
                cut = slice(n * second, (n + 1) * second)
                out[0] = dot3(wh[cut, :], wl[cut, :], fh[...], fl[...])
        pltpu.emit_pipeline(body, grid=(step,), in_specs=[one_row] * 4, out_specs=[one_row] * 4)(
            piece(s0, c), piece(buf["end0"], c), piece(buf["other0"], c), piece(buf["far0"], c),
            piece(buf["y0"], c), piece(buf["w0"], c), piece(buf["sy"], c), piece(buf["sw"], c))

    def scatter_stage(c):
        def body(own, e, pown, pend, yo, ye, ao, af):
            place(0, own[0])
            place(1, e[0])
            place(2, pown[0])
            place(3, pend[0])
            for n in range(4):
                cut = slice(n * second, (n + 1) * second)
                gather[n] = dot3(wth[cut, :], wtl[cut, :], fh[...], fl[...])
            yo[0] = gather[z]
            ye[0] = gather[end]
            ao[0] = gather[other]
            af[0] = gather[far]
        pltpu.emit_pipeline(body, grid=(step,), in_specs=[one_row] * 4, out_specs=[one_row] * 4)(
            piece(s1, c), piece(buf["psie"], c), piece(buf["phi"], c), piece(buf["phie"], c),
            piece(buf["po"], c), piece(buf["pe"], c), piece(buf["ao"], c), piece(buf["af"], c))

    def end_sum_stage(c):
        def body(x, y, out):
            out[...] = x[...] + y[...]
        pltpu.emit_pipeline(body, grid=(2,), in_specs=[quarter] * 2, out_specs=[quarter])(
            piece(buf["pe"], c), piece(buf["ba1"], c), piece(buf["se"], c))

    def own_sum_stage(c, *terms):
        def body(*args):
            value = args[0][...]
            for term in args[1:-2]:
                value = value + term[...]
            args[-2][...] += value
            args[-1][...] += half_step * value
        pltpu.emit_pipeline(body, grid=(2,), in_specs=[quarter] * len(terms), out_specs=[quarter] * 2)(
            *[piece(buf[term], c) for term in terms], piece(slope.at[0], c), piece(following.at[0], c))

    ahead = min(3, nc)
    section_stage(0, step, step // 4)

    @pl.when(hub)
    def _():
        pl.semaphore_wait(barrier, wide + 1)
        zcopy(OWN, 0, s0, buf["other0"], other).start()

    @pl.when(jnp.logical_not(hub))
    def _():
        pl.semaphore_wait(barrier, wide)
        zcopy(END, 0, s0, buf["end0"], my_hub).start()
        for n, matrix in enumerate((k2, c2)):
            end_matrix(n, matrix).start()

    fetches = [
        pltpu.make_async_copy(matrix, held, ms.at[n])
        for n, (matrix, held) in enumerate(((k2, k2v), (c2, c2v), (k1, k1v), (c1, c1v), (k3, k3v), (c3, c3v)))
    ]
    for fetch in fetches:
        fetch.start()

    if nc > 1:
        section_stage(step, rows - step, step // 2)

        @pl.when(hub)
        def _():
            for c in range(1, ahead):
                zcopy(OWN, c, s0, buf["other0"], other).start()

        @pl.when(jnp.logical_not(hub))
        def _():
            for c in range(1, nc):
                zcopy(END, c, s0, buf["end0"], my_hub).start()

    section_swapped_stage()
    to_whole(TO_S1, buf["s1b"], buf["t1"])
    for fetch in fetches:
        fetch.wait()
    for matrix, high, low in ((c1v, c1h, c1l), (c3v, c3h, c3l), (k1v, k1h, k1l), (k3v, k3h, k3l)):
        high[...], low[...] = halves(matrix[...])

    @pl.when(hub)
    def _():
        for n, (matrix, held) in enumerate(((k2, k2v), (c2, c2v))):
            end_matrix(n, matrix).wait_recv()
            for m, rows_of in enumerate((held, wend.at[n])):
                cut = slice((2 * n + m) * second, (2 * n + m + 1) * second)
                value = rows_of[...]
                wh[cut, :], wl[cut, :] = halves(value)
                wth[:, cut], wtl[:, cut] = halves(value.T)

    first_at = min(3, nc - 1)
    phi_at = min(5, nc - 1)
    base_at = nc
    coupled_at = nc + 1
    second_at = min(nc + 4, 2 * nc)
    last_at = max(2 * nc - 2, second_at)
    early = nc // 2

    def body(t, carry):
        @pl.when(jnp.logical_and(hub, t + ahead < nc))
        def _():
            zcopy(OWN, t + ahead, s0, buf["other0"], other).start()

        @pl.when(jnp.logical_and(hub, t < nc))
        def _():
            zrecv(END, t, buf["end0"])
            zcopy(FWD, t, buf["end0"], buf["far0"], other).start()

        @pl.when(t == first_at)
        def _():
            to_whole_wait(TO_S1, buf["t1"])
            first_stage([(buf["t1"], c1h, c1l)], buf["rc"])
            from_whole(BACK_C, buf["rc"], buf["bc"])

            @pl.when(jnp.logical_not(hub))
            def _():
                for c in range(early):
                    zcopy(PSI, c, s1, buf["psie"], my_hub).start()
            first_stage([(buf["t1"], k1h, k1l)], buf["rk"])
            transpose_stage(s0, buf["s0b"])

        @pl.when(t == phi_at)
        def _():
            from_whole_wait(BACK_C, buf["bc"])
            phi_stage(buf["bc"], buf["phi"])

            @pl.when(jnp.logical_not(hub))
            def _():
                for c in range(nc):
                    if c >= early:
                        zcopy(PSI, c, s1, buf["psie"], my_hub).start()
                    zcopy(PHI, c, buf["phi"], buf["phie"], my_hub).start()
            from_whole(BACK_K, buf["rk"], buf["bk"])
            to_whole(TO_S0, buf["s0b"], buf["t0"])

        @pl.when(jnp.logical_and(hub, jnp.logical_and(t >= nc - 1, t <= 2 * nc - 2)))
        def _():
            c = t - (nc - 1)
            zrecv(PSI, c, buf["psie"])
            zrecv(PHI, c, buf["phie"])
            scatter_stage(c)
            zcopy(SUM_F, c, buf["af"], buf["ba1"], other).start()

            @pl.when(jnp.logical_and(c == nc - 1, nc > 1))
            def _():
                zcopy(SUM_O, max(nc - 2, 0), buf["ao"], buf["ba0"], other).start()

            @pl.when(c != nc - 2)
            def _():
                zcopy(SUM_O, c, buf["ao"], buf["ba0"], other).start()

        @pl.when(jnp.logical_and(hub, jnp.logical_and(t >= 1, t <= nc)))
        def _():
            c = t - 1
            zrecv(OWN, c, buf["other0"])
            zrecv(FWD, c, buf["far0"])
            gather_stage(c)
            zcopy(WROW, c, buf["sw"], buf["w0"], end).start()
            zcopy(YROW, c, buf["sy"], buf["y0"], end).start()

        @pl.when(jnp.logical_and(hub, t >= nc + 1))
        def _():
            c = t - (nc + 1)
            here = jnp.where(c == nc - 2, 2, jnp.where(c == nc - 1, 1 if nc == 1 else 0, 1))

            def far_sum(e, carry):
                zrecv(SUM_F, e, buf["ba1"])
                end_sum_stage(e)
                zcopy(YEND, e, buf["se"], buf["y1"], end).start()
                return carry
            lax.fori_loop(c, c + here, far_sum, 0)
            zrecv(SUM_O, c, buf["ba0"])
            own_sum_stage(c, "po", "ba0")

        @pl.when(t == base_at)
        def _():
            from_whole_wait(BACK_K, buf["bk"])
            base_stage(s1, buf["bk"], wave.at[0], 1.0, 0)

        @pl.when(t == coupled_at)
        def _():
            @pl.when(jnp.logical_not(hub))
            def _():
                each_chunk(lambda c: zrecv(WROW, c, buf["w0"]))
            coupled_stage(buf["w0"], buf["w0b"])
            to_whole(TO_W0, buf["w0b"], buf["tw"])

        @pl.when(t == second_at)
        def _():
            to_whole_wait(TO_S0, buf["t0"])
            to_whole_wait(TO_W0, buf["tw"])
            first_stage([(buf["t0"], k1h, k1l), (buf["tw"], c1h, c1l)], buf["r0"])
            from_whole(BACK_0, buf["r0"], buf["b0"])

        @pl.when(t == last_at)
        def _():
            @pl.when(jnp.logical_not(hub))
            def _():
                each_chunk(lambda c: zrecv(YROW, c, buf["y0"]))
            from_whole_wait(BACK_0, buf["b0"])
            base_stage(s0, buf["b0"], wave.at[1], -1.0, 1, buf["y0"])
        return carry

    lax.fori_loop(0, 2 * nc + 1, body, 0)

    @pl.when(hub)
    def _():
        def sent(c):
            for kind, name in ((OWN, "s0"), (FWD, "end0"), (YROW, "sy"), (WROW, "sw"), (SUM_O, "ao"), (SUM_F, "af"), (YEND, "se")):
                zsent(kind, c, buf[name])
        each_chunk(sent)

    @pl.when(jnp.logical_not(hub))
    def _():
        def sent(c):
            zsent(END, c, s0)
            zsent(PSI, c, s1)
            zsent(PHI, c, buf["phi"])
            zrecv(YEND, c, buf["y1"])
            own_sum_stage(c, "y1")
        each_chunk(sent)
        for n, matrix in enumerate((k2, c2)):
            end_matrix(n, matrix).wait_send()

    for kind, name in ((TO_S1, "s1b"), (BACK_C, "rc"), (BACK_K, "rk"), (TO_S0, "s0b"), (TO_W0, "w0b"), (BACK_0, "r0")):
        wide_sent(kind, buf[name])


def write_kernel(results, slope_out, following_out, sems):
    copies = [
        pltpu.make_async_copy(results.at[pl.ds(0, 2)], slope_out, sems.at[0]),
        pltpu.make_async_copy(results.at[pl.ds(2, 2)], following_out, sems.at[1]),
    ]
    for copy in copies:
        copy.start()
    for copy in copies:
        copy.wait()


def local(wide, wavefunction, previous_slope, potential, kinetic_one, coupling_one, kinetic_two, coupling_two, kinetic_three, coupling_three):
    _, rows, second, third = wavefunction.shape
    full = rows * wide
    q = second // wide
    shapes = []
    for name in BUFFERS:
        if name in WIDE_SHAPED:
            shape = (q, full, third)
        elif name in SECOND_FIRST:
            shape = (second, rows, third)
        else:
            shape = (rows, second, third)
        shapes.append(jax.ShapeDtypeStruct(shape, jnp.float32))
    shapes += [pltpu.VMEM((4, rows, second, third), jnp.float32)]
    nc = rows // 8
    bf = jnp.bfloat16
    everything = 4 * second
    outs = pl.pallas_call(
        functools.partial(kernel, wide),
        out_shape=shapes,
        in_specs=[pl.BlockSpec(memory_space=pl.ANY)] * 9,
        out_specs=[pl.BlockSpec(memory_space=pl.ANY)] * len(BUFFERS) + [pl.BlockSpec(memory_space=pltpu.VMEM)],
        scratch_shapes=[pltpu.VMEM((everything, everything), bf)] * 4
        + [pltpu.VMEM((full, full), bf)] * 4
        + [pltpu.VMEM((third, third), bf)] * 4
        + [
            pltpu.VMEM((everything, third), bf),
            pltpu.VMEM((everything, third), bf),
            pltpu.VMEM((4, second, third), jnp.float32),
            pltpu.VMEM((2, second, everything), jnp.float32),
        ]
        + [pltpu.VMEM((second, everything), jnp.float32)] * 2
        + [pltpu.VMEM((full, full), jnp.float32)] * 2
        + [pltpu.VMEM((third, third), jnp.float32)] * 2
        + [
            pltpu.SemaphoreType.DMA((10, nc)),
            pltpu.SemaphoreType.DMA((10, nc)),
            pltpu.SemaphoreType.DMA((2,)),
            pltpu.SemaphoreType.DMA((2,)),
            pltpu.SemaphoreType.DMA((6,)),
            pltpu.SemaphoreType.DMA((6,)),
            pltpu.SemaphoreType.DMA((6,)),
            pltpu.SemaphoreType.DMA((6,)),
        ],
        compiler_params=pltpu.CompilerParams(collective_id=0, has_side_effects=True, vmem_limit_bytes=26 * 2**20),
        cost_estimate=pl.CostEstimate(flops=6 * 3584 * 2 * rows * second * third * 2, bytes_accessed=40 * rows * second * third * 4, transcendentals=0),
    )(wavefunction, previous_slope, potential, kinetic_two, coupling_two, kinetic_one, coupling_one, kinetic_three, coupling_three)
    return pl.pallas_call(
        write_kernel,
        in_specs=[pl.BlockSpec(memory_space=pltpu.VMEM)],
        out_specs=[pl.BlockSpec(memory_space=pl.ANY)] * 2,
        out_shape=[jax.ShapeDtypeStruct(wavefunction.shape, jnp.float32)] * 2,
        scratch_shapes=[pltpu.SemaphoreType.DMA((2,))],
        compiler_params=pltpu.CompilerParams(vmem_limit_bytes=2**20),
        cost_estimate=pl.CostEstimate(flops=0, bytes_accessed=wavefunction.size * 8, transcendentals=0),
    )(*outs[len(BUFFERS):])


def solution(mesh):
    wide = mesh.shape["wide"]
    field = P(None, "wide", "narrow", None)
    in_specs = (field, field, P("wide", "narrow", None), P(), P(), P("narrow", None), P("narrow", None), P(), P())

    def body(*arrays):
        return tuple(local(wide, *arrays))

    def run(*arrays):
        with jax.sharding.use_abstract_mesh(mesh.abstract_mesh):
            return jax.shard_map(body, mesh=mesh, in_specs=in_specs, out_specs=(field, field), check_vma=False)(*arrays)

    return run
```

```python
import functools

import jax
import jax.numpy as jnp
from jax import lax
from jax.experimental import pallas as pl
from jax.experimental.pallas import tpu as pltpu
from jax.sharding import PartitionSpec as P

half_step = 0.1
MESH = pl.DeviceIdType.MESH
OWN, END, FWD, YROW, WROW, PSI, PHI, SUM_O, SUM_F, YEND = range(10)
TO_S1, BACK_C, BACK_K, TO_S0, TO_W0, BACK_0 = range(6)
BUFFERS = (
    "end0", "other0", "far0", "y0", "w0", "sy", "sw",
    "s0b", "t0", "w0b", "tw", "r0", "b0",
    "s1b", "t1", "rc", "rk", "bc", "bk", "phi",
    "psie", "phie", "po", "pe", "ao", "af", "ba0", "ba1", "se", "y1", "s0", "s1",
)
WIDE_SHAPED = ("t0", "tw", "r0", "t1", "rc", "rk")
SECOND_FIRST = ("s0b", "w0b", "b0", "s1b", "bc", "bk")


def halves(x):
    high = x.astype(jnp.bfloat16)
    return high, (x - high.astype(jnp.float32)).astype(jnp.bfloat16)


def dot3(ah, al, bh, bl):
    dot = functools.partial(jnp.dot, preferred_element_type=jnp.float32)
    return dot(ah, bh) + dot(ah, bl) + dot(al, bh)


def kernel(wide, wave, prev, pot, k2, c2, k1, c1, k3, c3, *refs):
    buf = dict(zip(BUFFERS, refs[:len(BUFFERS)]))
    (results, wh, wl, wth, wtl, k1h, k1l, c1h, c1l, k3h, k3l, c3h, c3l, fh, fl, gather, wend, land,
     k2v, c2v, k1v, c1v, k3v, c3v, zs, zr, es, er, ms, ws, wr, wloc) = refs[len(BUFFERS):]
    rows, second, third = wave.shape[1:]
    full = rows * wide
    q = second // wide
    step = 8
    nc = rows // step
    me = lax.axis_index("wide")
    z = lax.axis_index("narrow")
    hub = jnp.logical_or(z == 1, z == 2)
    end = jnp.where(z == 1, 0, 3)
    other = 3 - z
    far = 3 - end
    my_hub = jnp.where(z == 0, 1, 2)
    slope, following = results.at[pl.ds(0, 2)], results.at[pl.ds(2, 2)]
    s0, s1 = buf["s0"], buf["s1"]

    def peer_of(d):
        return lax.rem(me + d, wide)

    barrier = pltpu.get_barrier_semaphore()

    def greet(d, carry):
        pl.semaphore_signal(barrier, inc=1, device_id={"wide": peer_of(d)}, device_id_type=MESH)
        return carry

    lax.fori_loop(1, wide, greet, 0)

    @pl.when(hub)
    def _():
        pl.semaphore_signal(barrier, inc=1, device_id={"narrow": end}, device_id_type=MESH)
        pl.semaphore_signal(barrier, inc=1, device_id={"narrow": other}, device_id_type=MESH)

    @pl.when(jnp.logical_not(hub))
    def _():
        pl.semaphore_signal(barrier, inc=1, device_id={"narrow": my_hub}, device_id_type=MESH)

    def piece(ref, c):
        return ref.at[pl.ds(pl.multiple_of(c * step, step), step)]

    def zcopy(kind, c, src, dst, target):
        return pltpu.make_async_remote_copy(
            src_ref=piece(src, c), dst_ref=piece(dst, c), send_sem=zs.at[kind, c], recv_sem=zr.at[kind, c],
            device_id={"narrow": target}, device_id_type=MESH)

    def zrecv(kind, c, dst):
        pltpu.make_async_copy(piece(dst, c), piece(dst, c), zr.at[kind, c]).wait()

    def zsent(kind, c, src):
        pltpu.make_async_copy(piece(src, c), piece(src, c), zs.at[kind, c]).wait()

    def end_matrix(n, matrix):
        return pltpu.make_async_remote_copy(
            src_ref=matrix, dst_ref=wend.at[n], send_sem=es.at[n], recv_sem=er.at[n],
            device_id={"narrow": my_hub}, device_id_type=MESH)

    def last_near():
        return pltpu.make_async_remote_copy(
            src_ref=buf["ao"].at[pl.ds(rows - step, step)], dst_ref=land, send_sem=zs.at[SUM_O, nc - 1],
            recv_sem=zr.at[SUM_O, nc - 1], device_id={"narrow": other}, device_id_type=MESH)

    def each_chunk(f):
        def body(c, carry):
            f(c)
            return carry
        lax.fori_loop(0, nc, body, 0)

    def mine_of(ref, index, size):
        return ref.at[:, pl.ds(pl.multiple_of(index * size, size), size)]

    def to_whole(kind, src, dst):
        def send(d, carry):
            p = peer_of(d)
            pltpu.make_async_remote_copy(
                src_ref=src.at[pl.ds(p * q, q)], dst_ref=mine_of(dst, me, rows),
                send_sem=ws.at[kind], recv_sem=wr.at[kind], device_id={"wide": p}, device_id_type=MESH).start()
            return carry
        lax.fori_loop(1, wide, send, 0)
        pltpu.make_async_copy(src.at[pl.ds(me * q, q)], mine_of(dst, me, rows), wloc.at[kind]).start()

    def to_whole_wait(kind, dst):
        part = dst.at[:, pl.ds(0, (wide - 1) * rows)]
        pltpu.make_async_copy(part, part, wr.at[kind]).wait()
        own = dst.at[:, pl.ds(0, rows)]
        pltpu.make_async_copy(own, own, wloc.at[kind]).wait()

    def from_whole(kind, src, dst):
        def send(d, carry):
            p = peer_of(d)
            pltpu.make_async_remote_copy(
                src_ref=mine_of(src, p, rows), dst_ref=dst.at[pl.ds(me * q, q)],
                send_sem=ws.at[kind], recv_sem=wr.at[kind], device_id={"wide": p}, device_id_type=MESH).start()
            return carry
        lax.fori_loop(1, wide, send, 0)
        pltpu.make_async_copy(mine_of(src, me, rows), dst.at[pl.ds(me * q, q)], wloc.at[kind]).start()

    def from_whole_wait(kind, dst):
        part = dst.at[pl.ds(0, (wide - 1) * q)]
        pltpu.make_async_copy(part, part, wr.at[kind]).wait()
        own = dst.at[pl.ds(0, q)]
        pltpu.make_async_copy(own, own, wloc.at[kind]).wait()

    def wide_sent(kind, src):
        part = src.at[pl.ds(0, (wide - 1) * q)] if src.shape[0] == second else src.at[:, pl.ds(0, (wide - 1) * rows)]
        pltpu.make_async_copy(part, part, ws.at[kind]).wait()

    by_first = pl.BlockSpec((step, second, third), lambda i: (i, 0, 0))
    by_second = pl.BlockSpec((second, step, third), lambda i: (0, i, 0))
    one_row = pl.BlockSpec((1, second, third), lambda i: (i, 0, 0))
    one_whole = pl.BlockSpec((1, full, third), lambda i: (i, 0, 0))

    parts = 2
    half_first = pl.BlockSpec((step, second // parts, third), lambda i, j: (i, j, 0))
    half_second = pl.BlockSpec((second // parts, step, third), lambda i, j: (j, i, 0))
    quarter = pl.BlockSpec((step // 2, second, third), lambda i: (i, 0, 0))

    def transpose_stage(src, dst):
        def body(x, out):
            for g in range(second // 8):
                out[8 * g:8 * g + 8, :, :] = jnp.swapaxes(x[:, 8 * g:8 * g + 8, :], 0, 1)
        pltpu.emit_pipeline(body, grid=(nc,), in_specs=[by_first], out_specs=[by_second])(src, dst)

    def section_stage(start, size, block):
        spec = pl.BlockSpec((block, second, third), lambda i: (i, 0, 0))

        def body(x, y, out):
            out[...] = x[...] + half_step * y[...]
        cut = pl.ds(start, size)
        pltpu.emit_pipeline(body, grid=(size // block,), in_specs=[spec] * 2, out_specs=[spec])(
            wave.at[0, cut], prev.at[0, cut], s0.at[cut])

    def section_swapped_stage():
        def body(x, y, out, out_swapped):
            for g in range(second // 8):
                cut = slice(8 * g, 8 * g + 8)
                value = x[:, cut, :] + half_step * y[:, cut, :]
                out[:, cut, :] = value
                out_swapped[cut, :, :] = jnp.swapaxes(value, 0, 1)
        pltpu.emit_pipeline(body, grid=(nc,), in_specs=[by_first] * 2, out_specs=[by_first, by_second])(
            wave.at[1], prev.at[1], s1, buf["s1b"])

    def third_dot(x, mh, ml):
        xh, xl = halves(x)
        return dot3(xh, xl, mh[...], ml[...])

    group = 32

    def phi_stage(src, dst):
        def body(x, out):
            for g in range(second // group):
                block = x[group * g:group * (g + 1)].reshape(group * step, third)
                result = third_dot(block, c3h, c3l).reshape(group, step, third)
                out[:, group * g:group * (g + 1), :] = jnp.swapaxes(result, 0, 1)
        pltpu.emit_pipeline(body, grid=(nc,), in_specs=[by_second], out_specs=[by_first])(src, dst)

    def coupled_stage(src, dst):
        def body(x, out):
            for g in range(second // group):
                block = x[:, group * g:group * (g + 1), :].reshape(group * step, third)
                result = third_dot(block, c3h, c3l).reshape(step, group, third)
                out[group * g:group * (g + 1), :, :] = jnp.swapaxes(result, 0, 1)
        pltpu.emit_pipeline(body, grid=(nc,), in_specs=[by_first], out_specs=[by_second])(src, dst)

    def base_stage(field, returned, start, sign, slot, extra=None):
        def body(x, v, back, base, *rest):
            out, out_next = rest[-2:]
            for g in range(second // parts // group):
                cut = slice(group * g, group * (g + 1))
                block = x[:, cut, :].reshape(group * step, third)
                result = third_dot(block, k3h, k3l).reshape(step, group, third)
                result = result + v[:, cut, :] * x[:, cut, :] + jnp.swapaxes(back[cut], 0, 1)
                if extra is not None:
                    result = result + rest[0][:, cut, :]
                result = sign * result
                out[:, cut, :] = result
                out_next[:, cut, :] = base[:, cut, :] + half_step * result
        ins = [field, pot, returned, start] + ([] if extra is None else [extra])
        specs = [half_first, half_first, half_second, half_first] + ([] if extra is None else [half_first])
        pltpu.emit_pipeline(body, grid=(nc, parts), in_specs=specs, out_specs=[half_first] * 2)(
            *ins, slope.at[slot], following.at[slot])

    def first_stage(terms, dst):
        def body(*args):
            out = args[-1]
            total = None
            for (_, mh, ml), x in zip(terms, args[:-1]):
                xh, xl = halves(x[0])
                value = dot3(mh[...], ml[...], xh, xl)
                total = value if total is None else total + value
            out[0] = total
        pltpu.emit_pipeline(body, grid=(q,), in_specs=[one_whole] * len(terms), out_specs=[one_whole])(
            *[t[0] for t in terms], dst)

    def place(slot, x):
        at = pl.ds(pl.multiple_of(slot * second, second), second)
        high, low = halves(x)
        fh[at, :] = high
        fl[at, :] = low

    def gather_stage(c):
        def body(own, e, o, f, y, v, ye, ve):
            place(z, own[0])
            place(end, e[0])
            place(other, o[0])
            place(far, f[0])
            for n, out in enumerate((y, ye, v, ve)):
                cut = slice(n * second, (n + 1) * second)
                out[0] = dot3(wh[cut, :], wl[cut, :], fh[...], fl[...])
        pltpu.emit_pipeline(body, grid=(step,), in_specs=[one_row] * 4, out_specs=[one_row] * 4)(
            piece(s0, c), piece(buf["end0"], c), piece(buf["other0"], c), piece(buf["far0"], c),
            piece(buf["y0"], c), piece(buf["w0"], c), piece(buf["sy"], c), piece(buf["sw"], c))

    def scatter_stage(c):
        def body(own, e, pown, pend, yo, ye, ao, af):
            place(0, own[0])
            place(1, e[0])
            place(2, pown[0])
            place(3, pend[0])
            for n in range(4):
                cut = slice(n * second, (n + 1) * second)
                gather[n] = dot3(wth[cut, :], wtl[cut, :], fh[...], fl[...])
            yo[0] = gather[z]
            ye[0] = gather[end]
            ao[0] = gather[other]
            af[0] = gather[far]
        pltpu.emit_pipeline(body, grid=(step,), in_specs=[one_row] * 4, out_specs=[one_row] * 4)(
            piece(s1, c), piece(buf["psie"], c), piece(buf["phi"], c), piece(buf["phie"], c),
            piece(buf["po"], c), piece(buf["pe"], c), piece(buf["ao"], c), piece(buf["af"], c))

    def end_sum_stage(c):
        def body(x, y, out):
            out[...] = x[...] + y[...]
        pltpu.emit_pipeline(body, grid=(2,), in_specs=[quarter] * 2, out_specs=[quarter])(
            piece(buf["pe"], c), piece(buf["ba1"], c), piece(buf["se"], c))

    def own_sum_stage(c, *terms):
        def body(*args):
            value = args[0][...]
            for term in args[1:-2]:
                value = value + term[...]
            args[-2][...] += value
            args[-1][...] += half_step * value
        pltpu.emit_pipeline(body, grid=(2,), in_specs=[quarter] * len(terms), out_specs=[quarter] * 2)(
            *[piece(buf[term], c) for term in terms], piece(slope.at[0], c), piece(following.at[0], c))

    ahead = min(3, nc)
    small = step // 4

    def first_piece(i):
        at = pl.ds(i * small, small)
        pltpu.make_async_remote_copy(
            src_ref=s0.at[at], dst_ref=buf["other0"].at[at], send_sem=zs.at[OWN, 0], recv_sem=zr.at[OWN, 0],
            device_id={"narrow": other}, device_id_type=MESH).start()

    section_stage(0, small, small)

    @pl.when(hub)
    def _():
        pl.semaphore_wait(barrier, wide + 1)
        first_piece(0)

    @pl.when(jnp.logical_not(hub))
    def _():
        pl.semaphore_wait(barrier, wide)

    def next_piece(i, carry):
        section_stage(i * small, small, small)

        @pl.when(hub)
        def _():
            first_piece(i)
        return carry
    lax.fori_loop(1, step // small, next_piece, 0)

    @pl.when(jnp.logical_not(hub))
    def _():
        zcopy(END, 0, s0, buf["end0"], my_hub).start()
        for n, matrix in enumerate((k2, c2)):
            end_matrix(n, matrix).start()

    fetches = [
        pltpu.make_async_copy(matrix, held, ms.at[n])
        for n, (matrix, held) in enumerate(((k2, k2v), (c2, c2v), (k1, k1v), (c1, c1v), (k3, k3v), (c3, c3v)))
    ]
    for fetch in fetches:
        fetch.start()

    if nc > 1:
        section_stage(step, rows - step, step // 2)

        @pl.when(hub)
        def _():
            for c in range(1, ahead):
                zcopy(OWN, c, s0, buf["other0"], other).start()

        @pl.when(jnp.logical_not(hub))
        def _():
            for c in range(1, nc):
                zcopy(END, c, s0, buf["end0"], my_hub).start()

    section_swapped_stage()
    to_whole(TO_S1, buf["s1b"], buf["t1"])
    for fetch in fetches:
        fetch.wait()
    for matrix, high, low in ((c1v, c1h, c1l), (c3v, c3h, c3l), (k1v, k1h, k1l), (k3v, k3h, k3l)):
        high[...], low[...] = halves(matrix[...])

    @pl.when(hub)
    def _():
        for n, (matrix, held) in enumerate(((k2, k2v), (c2, c2v))):
            end_matrix(n, matrix).wait_recv()
            for m, rows_of in enumerate((held, wend.at[n])):
                cut = slice((2 * n + m) * second, (2 * n + m + 1) * second)
                value = rows_of[...]
                wh[cut, :], wl[cut, :] = halves(value)
                wth[:, cut], wtl[:, cut] = halves(value.T)

    first_at = min(3, nc - 1)
    phi_at = min(5, nc - 1)
    base_at = nc
    coupled_at = nc + 1
    second_at = min(nc + 4, 2 * nc)
    last_at = max(2 * nc - 2, second_at)
    early = nc // 2

    def body(t, carry):
        @pl.when(jnp.logical_and(hub, t + ahead < nc))
        def _():
            zcopy(OWN, t + ahead, s0, buf["other0"], other).start()

        @pl.when(jnp.logical_and(hub, t < nc))
        def _():
            zrecv(END, t, buf["end0"])
            zcopy(FWD, t, buf["end0"], buf["far0"], other).start()

        @pl.when(t == first_at)
        def _():
            to_whole_wait(TO_S1, buf["t1"])
            first_stage([(buf["t1"], c1h, c1l)], buf["rc"])
            from_whole(BACK_C, buf["rc"], buf["bc"])

            @pl.when(jnp.logical_not(hub))
            def _():
                for c in range(early):
                    zcopy(PSI, c, s1, buf["psie"], my_hub).start()
            first_stage([(buf["t1"], k1h, k1l)], buf["rk"])
            transpose_stage(s0, buf["s0b"])

        @pl.when(t == phi_at)
        def _():
            from_whole_wait(BACK_C, buf["bc"])
            phi_stage(buf["bc"], buf["phi"])

            @pl.when(jnp.logical_not(hub))
            def _():
                for c in range(nc):
                    if c >= early:
                        zcopy(PSI, c, s1, buf["psie"], my_hub).start()
                    zcopy(PHI, c, buf["phi"], buf["phie"], my_hub).start()
            from_whole(BACK_K, buf["rk"], buf["bk"])
            to_whole(TO_S0, buf["s0b"], buf["t0"])

        @pl.when(jnp.logical_and(hub, jnp.logical_and(t >= nc - 1, t <= 2 * nc - 2)))
        def _():
            c = t - (nc - 1)
            zrecv(PSI, c, buf["psie"])
            zrecv(PHI, c, buf["phie"])
            scatter_stage(c)
            zcopy(SUM_F, c, buf["af"], buf["ba1"], other).start()

            @pl.when(jnp.logical_and(c == nc - 1, nc > 1))
            def _():
                zcopy(SUM_O, max(nc - 2, 0), buf["ao"], buf["ba0"], other).start()

            @pl.when(c == nc - 1)
            def _():
                last_near().start()

            @pl.when(c < nc - 2)
            def _():
                zcopy(SUM_O, c, buf["ao"], buf["ba0"], other).start()

        @pl.when(jnp.logical_and(hub, jnp.logical_and(t >= 1, t <= nc)))
        def _():
            c = t - 1
            zrecv(OWN, c, buf["other0"])
            zrecv(FWD, c, buf["far0"])
            gather_stage(c)
            zcopy(WROW, c, buf["sw"], buf["w0"], end).start()
            zcopy(YROW, c, buf["sy"], buf["y0"], end).start()

        @pl.when(jnp.logical_and(hub, t >= nc + 1))
        def _():
            c = t - (nc + 1)
            here = jnp.where(c == nc - 2, 2, jnp.where(c == nc - 1, 1 if nc == 1 else 0, 1))

            def far_sum(e, carry):
                zrecv(SUM_F, e, buf["ba1"])
                end_sum_stage(e)
                zcopy(YEND, e, buf["se"], buf["y1"], end).start()
                return carry
            lax.fori_loop(c, c + here, far_sum, 0)

            @pl.when(c < nc - 1)
            def _():
                zrecv(SUM_O, c, buf["ba0"])
                own_sum_stage(c, "po", "ba0")

            @pl.when(c == nc - 1)
            def _():
                own_sum_stage(c, "po")

        @pl.when(t == base_at)
        def _():
            from_whole_wait(BACK_K, buf["bk"])
            base_stage(s1, buf["bk"], wave.at[0], 1.0, 0)

        @pl.when(t == coupled_at)
        def _():
            @pl.when(jnp.logical_not(hub))
            def _():
                each_chunk(lambda c: zrecv(WROW, c, buf["w0"]))
            coupled_stage(buf["w0"], buf["w0b"])
            to_whole(TO_W0, buf["w0b"], buf["tw"])

        @pl.when(t == second_at)
        def _():
            to_whole_wait(TO_S0, buf["t0"])
            to_whole_wait(TO_W0, buf["tw"])
            first_stage([(buf["t0"], k1h, k1l), (buf["tw"], c1h, c1l)], buf["r0"])
            from_whole(BACK_0, buf["r0"], buf["b0"])

        @pl.when(t == last_at)
        def _():
            @pl.when(jnp.logical_not(hub))
            def _():
                each_chunk(lambda c: zrecv(YROW, c, buf["y0"]))
            from_whole_wait(BACK_0, buf["b0"])
            base_stage(s0, buf["b0"], wave.at[1], -1.0, 1, buf["y0"])
        return carry

    lax.fori_loop(0, 2 * nc + 1, body, 0)

    for kind, name in ((TO_S1, "s1b"), (BACK_C, "rc"), (BACK_K, "rk"), (TO_S0, "s0b"), (TO_W0, "w0b"), (BACK_0, "r0")):
        wide_sent(kind, buf[name])

    @pl.when(hub)
    def _():
        def sent(c):
            for kind, name in ((OWN, "s0"), (FWD, "end0"), (YROW, "sy"), (WROW, "sw"), (SUM_F, "af"), (YEND, "se")):
                zsent(kind, c, buf[name])

            @pl.when(c < nc - 1)
            def _():
                zsent(SUM_O, c, buf["ao"])
        each_chunk(sent)
        last_near().wait_recv()
        tail = slice(rows - step, rows)
        value = land[...]
        results[0, tail] = results[0, tail] + value
        results[2, tail] = results[2, tail] + half_step * value
        last_near().wait_send()

    @pl.when(jnp.logical_not(hub))
    def _():
        def sent(c):
            zsent(END, c, s0)
            zsent(PSI, c, s1)
            zsent(PHI, c, buf["phi"])
            zrecv(YEND, c, buf["y1"])
            own_sum_stage(c, "y1")
        each_chunk(sent)
        for n, matrix in enumerate((k2, c2)):
            end_matrix(n, matrix).wait_send()


def write_kernel(results, slope_out, following_out, sems):
    copies = [
        pltpu.make_async_copy(results.at[pl.ds(0, 2)], slope_out, sems.at[0]),
        pltpu.make_async_copy(results.at[pl.ds(2, 2)], following_out, sems.at[1]),
    ]
    for copy in copies:
        copy.start()
    for copy in copies:
        copy.wait()


def local(wide, wavefunction, previous_slope, potential, kinetic_one, coupling_one, kinetic_two, coupling_two, kinetic_three, coupling_three):
    _, rows, second, third = wavefunction.shape
    full = rows * wide
    q = second // wide
    shapes = []
    for name in BUFFERS:
        if name in WIDE_SHAPED:
            shape = (q, full, third)
        elif name in SECOND_FIRST:
            shape = (second, rows, third)
        else:
            shape = (rows, second, third)
        shapes.append(jax.ShapeDtypeStruct(shape, jnp.float32))
    shapes += [pltpu.VMEM((4, rows, second, third), jnp.float32)]
    nc = rows // 8
    bf = jnp.bfloat16
    everything = 4 * second
    outs = pl.pallas_call(
        functools.partial(kernel, wide),
        out_shape=shapes,
        in_specs=[pl.BlockSpec(memory_space=pl.ANY)] * 9,
        out_specs=[pl.BlockSpec(memory_space=pl.ANY)] * len(BUFFERS) + [pl.BlockSpec(memory_space=pltpu.VMEM)],
        scratch_shapes=[pltpu.VMEM((everything, everything), bf)] * 4
        + [pltpu.VMEM((full, full), bf)] * 4
        + [pltpu.VMEM((third, third), bf)] * 4
        + [
            pltpu.VMEM((everything, third), bf),
            pltpu.VMEM((everything, third), bf),
            pltpu.VMEM((4, second, third), jnp.float32),
            pltpu.VMEM((2, second, everything), jnp.float32),
            pltpu.VMEM((8, second, third), jnp.float32),
        ]
        + [pltpu.VMEM((second, everything), jnp.float32)] * 2
        + [pltpu.VMEM((full, full), jnp.float32)] * 2
        + [pltpu.VMEM((third, third), jnp.float32)] * 2
        + [
            pltpu.SemaphoreType.DMA((10, nc)),
            pltpu.SemaphoreType.DMA((10, nc)),
            pltpu.SemaphoreType.DMA((2,)),
            pltpu.SemaphoreType.DMA((2,)),
            pltpu.SemaphoreType.DMA((6,)),
            pltpu.SemaphoreType.DMA((6,)),
            pltpu.SemaphoreType.DMA((6,)),
            pltpu.SemaphoreType.DMA((6,)),
        ],
        compiler_params=pltpu.CompilerParams(collective_id=0, has_side_effects=True, vmem_limit_bytes=26 * 2**20),
        cost_estimate=pl.CostEstimate(flops=6 * 3584 * 2 * rows * second * third * 2, bytes_accessed=40 * rows * second * third * 4, transcendentals=0),
    )(wavefunction, previous_slope, potential, kinetic_two, coupling_two, kinetic_one, coupling_one, kinetic_three, coupling_three)
    return pl.pallas_call(
        write_kernel,
        in_specs=[pl.BlockSpec(memory_space=pltpu.VMEM)],
        out_specs=[pl.BlockSpec(memory_space=pl.ANY)] * 2,
        out_shape=[jax.ShapeDtypeStruct(wavefunction.shape, jnp.float32)] * 2,
        scratch_shapes=[pltpu.SemaphoreType.DMA((2,))],
        compiler_params=pltpu.CompilerParams(vmem_limit_bytes=2**20),
        cost_estimate=pl.CostEstimate(flops=0, bytes_accessed=wavefunction.size * 8, transcendentals=0),
    )(*outs[len(BUFFERS):])


def solution(mesh):
    wide = mesh.shape["wide"]
    field = P(None, "wide", "narrow", None)
    in_specs = (field, field, P("wide", "narrow", None), P(), P(), P("narrow", None), P("narrow", None), P(), P())

    def body(*arrays):
        return tuple(local(wide, *arrays))

    def run(*arrays):
        with jax.sharding.use_abstract_mesh(mesh.abstract_mesh):
            return jax.shard_map(body, mesh=mesh, in_specs=in_specs, out_specs=(field, field), check_vma=False)(*arrays)

    return run
```

```python
import functools

import jax
import jax.numpy as jnp
from jax import lax
from jax.experimental import pallas as pl
from jax.experimental.pallas import tpu as pltpu
from jax.sharding import PartitionSpec as P

half_step = 0.1
MESH = pl.DeviceIdType.MESH
OWN, END, FWD, YROW, WROW, PSI, PHI, SUM_O, SUM_F, YEND = range(10)
late_rows = 4
TO_S1, BACK_C, BACK_K, TO_S0, TO_W0, BACK_0 = range(6)
BUFFERS = (
    "end0", "other0", "far0", "y0", "w0", "sy", "sw",
    "s0b", "t0", "w0b", "tw", "r0", "b0",
    "s1b", "t1", "rc", "rk", "bc", "bk", "phi",
    "psie", "phie", "po", "pe", "ao", "af", "ba0", "ba1", "se", "y1", "s0", "s1", "late", "held",
)
WIDE_SHAPED = ("t0", "tw", "r0", "t1", "rc", "rk")
SECOND_FIRST = ("s0b", "w0b", "b0", "s1b", "bc", "bk")


def halves(x):
    high = x.astype(jnp.bfloat16)
    return high, (x - high.astype(jnp.float32)).astype(jnp.bfloat16)


def dot3(ah, al, bh, bl):
    dot = functools.partial(jnp.dot, preferred_element_type=jnp.float32)
    return dot(ah, bh) + dot(ah, bl) + dot(al, bh)


def kernel(wide, wave, prev, pot, k2, c2, k1, c1, k3, c3, *refs):
    buf = dict(zip(BUFFERS, refs[:len(BUFFERS)]))
    (results, wh, wl, wth, wtl, k1h, k1l, c1h, c1l, k3h, k3l, c3h, c3l, fh, fl, gather, wend, land,
     k2v, c2v, k1v, c1v, k3v, c3v, zs, zr, es, er, ms, ls, ws, wr, wloc) = refs[len(BUFFERS):]
    rows, second, third = wave.shape[1:]
    full = rows * wide
    q = second // wide
    step = 8
    nc = rows // step
    me = lax.axis_index("wide")
    z = lax.axis_index("narrow")
    hub = jnp.logical_or(z == 1, z == 2)
    end = jnp.where(z == 1, 0, 3)
    other = 3 - z
    far = 3 - end
    my_hub = jnp.where(z == 0, 1, 2)
    slope, following = results.at[pl.ds(0, 2)], results.at[pl.ds(2, 2)]
    s0, s1 = buf["s0"], buf["s1"]

    def peer_of(d):
        return lax.rem(me + d, wide)

    barrier = pltpu.get_barrier_semaphore()

    def greet(d, carry):
        pl.semaphore_signal(barrier, inc=1, device_id={"wide": peer_of(d)}, device_id_type=MESH)
        return carry

    lax.fori_loop(1, wide, greet, 0)

    @pl.when(hub)
    def _():
        pl.semaphore_signal(barrier, inc=1, device_id={"narrow": end}, device_id_type=MESH)
        pl.semaphore_signal(barrier, inc=1, device_id={"narrow": other}, device_id_type=MESH)

    @pl.when(jnp.logical_not(hub))
    def _():
        pl.semaphore_signal(barrier, inc=1, device_id={"narrow": my_hub}, device_id_type=MESH)

    def piece(ref, c):
        return ref.at[pl.ds(pl.multiple_of(c * step, step), step)]

    def zcopy(kind, c, src, dst, target):
        return pltpu.make_async_remote_copy(
            src_ref=piece(src, c), dst_ref=piece(dst, c), send_sem=zs.at[kind, c], recv_sem=zr.at[kind, c],
            device_id={"narrow": target}, device_id_type=MESH)

    def zrecv(kind, c, dst):
        pltpu.make_async_copy(piece(dst, c), piece(dst, c), zr.at[kind, c]).wait()

    def zsent(kind, c, src):
        pltpu.make_async_copy(piece(src, c), piece(src, c), zs.at[kind, c]).wait()

    def end_matrix(n, matrix):
        return pltpu.make_async_remote_copy(
            src_ref=matrix, dst_ref=wend.at[n], send_sem=es.at[n], recv_sem=er.at[n],
            device_id={"narrow": my_hub}, device_id_type=MESH)

    def last_near():
        return pltpu.make_async_remote_copy(
            src_ref=buf["ao"].at[pl.ds(rows - step, step - late_rows)], dst_ref=land, send_sem=zs.at[SUM_O, nc - 1],
            recv_sem=zr.at[SUM_O, nc - 1], device_id={"narrow": other}, device_id_type=MESH)

    def held_copies():
        late = pl.ds(rows - late_rows, late_rows)
        return [
            pltpu.make_async_copy(slope.at[0, late], buf["held"].at[0], ls.at[1]),
            pltpu.make_async_copy(following.at[0, late], buf["held"].at[1], ls.at[2]),
        ]

    def late_copy():
        return pltpu.make_async_copy(buf["ao"].at[pl.ds(rows - late_rows, late_rows)], buf["late"], ls.at[0])

    def each_chunk(f):
        def body(c, carry):
            f(c)
            return carry
        lax.fori_loop(0, nc, body, 0)

    def mine_of(ref, index, size):
        return ref.at[:, pl.ds(pl.multiple_of(index * size, size), size)]

    def to_whole(kind, src, dst):
        def send(d, carry):
            p = peer_of(d)
            pltpu.make_async_remote_copy(
                src_ref=src.at[pl.ds(p * q, q)], dst_ref=mine_of(dst, me, rows),
                send_sem=ws.at[kind], recv_sem=wr.at[kind], device_id={"wide": p}, device_id_type=MESH).start()
            return carry
        lax.fori_loop(1, wide, send, 0)
        pltpu.make_async_copy(src.at[pl.ds(me * q, q)], mine_of(dst, me, rows), wloc.at[kind]).start()

    def to_whole_wait(kind, dst):
        part = dst.at[:, pl.ds(0, (wide - 1) * rows)]
        pltpu.make_async_copy(part, part, wr.at[kind]).wait()
        own = dst.at[:, pl.ds(0, rows)]
        pltpu.make_async_copy(own, own, wloc.at[kind]).wait()

    def from_whole(kind, src, dst):
        def send(d, carry):
            p = peer_of(d)
            pltpu.make_async_remote_copy(
                src_ref=mine_of(src, p, rows), dst_ref=dst.at[pl.ds(me * q, q)],
                send_sem=ws.at[kind], recv_sem=wr.at[kind], device_id={"wide": p}, device_id_type=MESH).start()
            return carry
        lax.fori_loop(1, wide, send, 0)
        pltpu.make_async_copy(mine_of(src, me, rows), dst.at[pl.ds(me * q, q)], wloc.at[kind]).start()

    def from_whole_wait(kind, dst):
        part = dst.at[pl.ds(0, (wide - 1) * q)]
        pltpu.make_async_copy(part, part, wr.at[kind]).wait()
        own = dst.at[pl.ds(0, q)]
        pltpu.make_async_copy(own, own, wloc.at[kind]).wait()

    def wide_sent(kind, src):
        part = src.at[pl.ds(0, (wide - 1) * q)] if src.shape[0] == second else src.at[:, pl.ds(0, (wide - 1) * rows)]
        pltpu.make_async_copy(part, part, ws.at[kind]).wait()

    by_first = pl.BlockSpec((step, second, third), lambda i: (i, 0, 0))
    by_second = pl.BlockSpec((second, step, third), lambda i: (0, i, 0))
    one_row = pl.BlockSpec((1, second, third), lambda i: (i, 0, 0))
    one_whole = pl.BlockSpec((1, full, third), lambda i: (i, 0, 0))

    parts = 2
    half_first = pl.BlockSpec((step, second // parts, third), lambda i, j: (i, j, 0))
    half_second = pl.BlockSpec((second // parts, step, third), lambda i, j: (j, i, 0))
    quarter = pl.BlockSpec((step // 2, second, third), lambda i: (i, 0, 0))

    def transpose_stage(src, dst):
        def body(x, out):
            for g in range(second // 8):
                out[8 * g:8 * g + 8, :, :] = jnp.swapaxes(x[:, 8 * g:8 * g + 8, :], 0, 1)
        pltpu.emit_pipeline(body, grid=(nc,), in_specs=[by_first], out_specs=[by_second])(src, dst)

    def section_stage(start, size, block):
        spec = pl.BlockSpec((block, second, third), lambda i: (i, 0, 0))

        def body(x, y, out):
            out[...] = x[...] + half_step * y[...]
        cut = pl.ds(start, size)
        pltpu.emit_pipeline(body, grid=(size // block,), in_specs=[spec] * 2, out_specs=[spec])(
            wave.at[0, cut], prev.at[0, cut], s0.at[cut])

    def section_swapped_stage():
        def body(x, y, out, out_swapped):
            for g in range(second // 8):
                cut = slice(8 * g, 8 * g + 8)
                value = x[:, cut, :] + half_step * y[:, cut, :]
                out[:, cut, :] = value
                out_swapped[cut, :, :] = jnp.swapaxes(value, 0, 1)
        pltpu.emit_pipeline(body, grid=(nc,), in_specs=[by_first] * 2, out_specs=[by_first, by_second])(
            wave.at[1], prev.at[1], s1, buf["s1b"])

    def third_dot(x, mh, ml):
        xh, xl = halves(x)
        return dot3(xh, xl, mh[...], ml[...])

    group = 32

    def phi_stage(src, dst):
        def body(x, out):
            for g in range(second // group):
                block = x[group * g:group * (g + 1)].reshape(group * step, third)
                result = third_dot(block, c3h, c3l).reshape(group, step, third)
                out[:, group * g:group * (g + 1), :] = jnp.swapaxes(result, 0, 1)
        pltpu.emit_pipeline(body, grid=(nc,), in_specs=[by_second], out_specs=[by_first])(src, dst)

    def coupled_stage(src, dst):
        def body(x, out):
            for g in range(second // group):
                block = x[:, group * g:group * (g + 1), :].reshape(group * step, third)
                result = third_dot(block, c3h, c3l).reshape(step, group, third)
                out[group * g:group * (g + 1), :, :] = jnp.swapaxes(result, 0, 1)
        pltpu.emit_pipeline(body, grid=(nc,), in_specs=[by_first], out_specs=[by_second])(src, dst)

    def base_stage(field, returned, start, sign, slot, extra=None):
        def body(x, v, back, base, *rest):
            out, out_next = rest[-2:]
            for g in range(second // parts // group):
                cut = slice(group * g, group * (g + 1))
                block = x[:, cut, :].reshape(group * step, third)
                result = third_dot(block, k3h, k3l).reshape(step, group, third)
                result = result + v[:, cut, :] * x[:, cut, :] + jnp.swapaxes(back[cut], 0, 1)
                if extra is not None:
                    result = result + rest[0][:, cut, :]
                result = sign * result
                out[:, cut, :] = result
                out_next[:, cut, :] = base[:, cut, :] + half_step * result
        ins = [field, pot, returned, start] + ([] if extra is None else [extra])
        specs = [half_first, half_first, half_second, half_first] + ([] if extra is None else [half_first])
        pltpu.emit_pipeline(body, grid=(nc, parts), in_specs=specs, out_specs=[half_first] * 2)(
            *ins, slope.at[slot], following.at[slot])

    def first_stage(terms, dst):
        def body(*args):
            out = args[-1]
            total = None
            for (_, mh, ml), x in zip(terms, args[:-1]):
                xh, xl = halves(x[0])
                value = dot3(mh[...], ml[...], xh, xl)
                total = value if total is None else total + value
            out[0] = total
        pltpu.emit_pipeline(body, grid=(q,), in_specs=[one_whole] * len(terms), out_specs=[one_whole])(
            *[t[0] for t in terms], dst)

    def place(slot, x):
        at = pl.ds(pl.multiple_of(slot * second, second), second)
        high, low = halves(x)
        fh[at, :] = high
        fl[at, :] = low

    def gather_stage(c):
        def body(own, e, o, f, y, v, ye, ve):
            place(z, own[0])
            place(end, e[0])
            place(other, o[0])
            place(far, f[0])
            for n, out in enumerate((y, ye, v, ve)):
                cut = slice(n * second, (n + 1) * second)
                out[0] = dot3(wh[cut, :], wl[cut, :], fh[...], fl[...])
        pltpu.emit_pipeline(body, grid=(step,), in_specs=[one_row] * 4, out_specs=[one_row] * 4)(
            piece(s0, c), piece(buf["end0"], c), piece(buf["other0"], c), piece(buf["far0"], c),
            piece(buf["y0"], c), piece(buf["w0"], c), piece(buf["sy"], c), piece(buf["sw"], c))

    def scatter_stage(c):
        def body(own, e, pown, pend, yo, ye, ao, af):
            place(0, own[0])
            place(1, e[0])
            place(2, pown[0])
            place(3, pend[0])
            for n in range(4):
                cut = slice(n * second, (n + 1) * second)
                gather[n] = dot3(wth[cut, :], wtl[cut, :], fh[...], fl[...])
            yo[0] = gather[z]
            ye[0] = gather[end]
            ao[0] = gather[other]
            af[0] = gather[far]
        pltpu.emit_pipeline(body, grid=(step,), in_specs=[one_row] * 4, out_specs=[one_row] * 4)(
            piece(s1, c), piece(buf["psie"], c), piece(buf["phi"], c), piece(buf["phie"], c),
            piece(buf["po"], c), piece(buf["pe"], c), piece(buf["ao"], c), piece(buf["af"], c))

    def end_sum_stage(c):
        def body(x, y, out):
            out[...] = x[...] + y[...]
        pltpu.emit_pipeline(body, grid=(2,), in_specs=[quarter] * 2, out_specs=[quarter])(
            piece(buf["pe"], c), piece(buf["ba1"], c), piece(buf["se"], c))

    def own_sum_stage(c, *terms):
        def body(*args):
            value = args[0][...]
            for term in args[1:-2]:
                value = value + term[...]
            args[-2][...] += value
            args[-1][...] += half_step * value
        pltpu.emit_pipeline(body, grid=(2,), in_specs=[quarter] * len(terms), out_specs=[quarter] * 2)(
            *[piece(buf[term], c) for term in terms], piece(slope.at[0], c), piece(following.at[0], c))

    ahead = min(3, nc)
    small = step // 4

    def first_piece(i):
        at = pl.ds(i * small, small)
        pltpu.make_async_remote_copy(
            src_ref=s0.at[at], dst_ref=buf["other0"].at[at], send_sem=zs.at[OWN, 0], recv_sem=zr.at[OWN, 0],
            device_id={"narrow": other}, device_id_type=MESH).start()

    section_stage(0, small, small)

    @pl.when(hub)
    def _():
        pl.semaphore_wait(barrier, wide + 1)
        first_piece(0)

    @pl.when(jnp.logical_not(hub))
    def _():
        pl.semaphore_wait(barrier, wide)

    def next_piece(i, carry):
        section_stage(i * small, small, small)

        @pl.when(hub)
        def _():
            first_piece(i)
        return carry
    lax.fori_loop(1, step // small, next_piece, 0)

    @pl.when(jnp.logical_not(hub))
    def _():
        zcopy(END, 0, s0, buf["end0"], my_hub).start()
        for n, matrix in enumerate((k2, c2)):
            end_matrix(n, matrix).start()

    fetches = [
        pltpu.make_async_copy(matrix, held, ms.at[n])
        for n, (matrix, held) in enumerate(((k2, k2v), (c2, c2v), (k1, k1v), (c1, c1v), (k3, k3v), (c3, c3v)))
    ]
    for fetch in fetches:
        fetch.start()

    if nc > 1:
        section_stage(step, rows - step, step // 2)

        @pl.when(hub)
        def _():
            for c in range(1, ahead):
                zcopy(OWN, c, s0, buf["other0"], other).start()

        @pl.when(jnp.logical_not(hub))
        def _():
            for c in range(1, nc):
                zcopy(END, c, s0, buf["end0"], my_hub).start()

    section_swapped_stage()
    to_whole(TO_S1, buf["s1b"], buf["t1"])
    for fetch in fetches:
        fetch.wait()
    for matrix, high, low in ((c1v, c1h, c1l), (c3v, c3h, c3l), (k1v, k1h, k1l), (k3v, k3h, k3l)):
        high[...], low[...] = halves(matrix[...])

    @pl.when(hub)
    def _():
        for n, (matrix, held) in enumerate(((k2, k2v), (c2, c2v))):
            end_matrix(n, matrix).wait_recv()
            for m, rows_of in enumerate((held, wend.at[n])):
                cut = slice((2 * n + m) * second, (2 * n + m + 1) * second)
                value = rows_of[...]
                wh[cut, :], wl[cut, :] = halves(value)
                wth[:, cut], wtl[:, cut] = halves(value.T)

    first_at = min(3, nc - 1)
    phi_at = min(5, nc - 1)
    base_at = nc
    coupled_at = nc + 1
    second_at = min(nc + 4, 2 * nc)
    last_at = max(2 * nc - 2, second_at)
    early = nc // 2

    def body(t, carry):
        @pl.when(jnp.logical_and(hub, t + ahead < nc))
        def _():
            zcopy(OWN, t + ahead, s0, buf["other0"], other).start()

        @pl.when(jnp.logical_and(hub, t < nc))
        def _():
            zrecv(END, t, buf["end0"])
            zcopy(FWD, t, buf["end0"], buf["far0"], other).start()

        @pl.when(t == first_at)
        def _():
            to_whole_wait(TO_S1, buf["t1"])
            first_stage([(buf["t1"], c1h, c1l)], buf["rc"])
            from_whole(BACK_C, buf["rc"], buf["bc"])

            @pl.when(jnp.logical_not(hub))
            def _():
                for c in range(early):
                    zcopy(PSI, c, s1, buf["psie"], my_hub).start()
            first_stage([(buf["t1"], k1h, k1l)], buf["rk"])
            transpose_stage(s0, buf["s0b"])

        @pl.when(t == phi_at)
        def _():
            from_whole_wait(BACK_C, buf["bc"])
            phi_stage(buf["bc"], buf["phi"])

            @pl.when(jnp.logical_not(hub))
            def _():
                for c in range(nc):
                    if c >= early:
                        zcopy(PSI, c, s1, buf["psie"], my_hub).start()
                    zcopy(PHI, c, buf["phi"], buf["phie"], my_hub).start()
            from_whole(BACK_K, buf["rk"], buf["bk"])
            to_whole(TO_S0, buf["s0b"], buf["t0"])

        @pl.when(jnp.logical_and(hub, jnp.logical_and(t >= nc - 1, t <= 2 * nc - 2)))
        def _():
            c = t - (nc - 1)
            zrecv(PSI, c, buf["psie"])
            zrecv(PHI, c, buf["phie"])
            scatter_stage(c)
            zcopy(SUM_F, c, buf["af"], buf["ba1"], other).start()

            @pl.when(jnp.logical_and(c == nc - 1, nc > 1))
            def _():
                zcopy(SUM_O, max(nc - 2, 0), buf["ao"], buf["ba0"], other).start()

            @pl.when(c == nc - 1)
            def _():
                last_near().start()
                late_copy().start()

            @pl.when(c < nc - 2)
            def _():
                zcopy(SUM_O, c, buf["ao"], buf["ba0"], other).start()

        @pl.when(jnp.logical_and(hub, jnp.logical_and(t >= 1, t <= nc)))
        def _():
            c = t - 1
            zrecv(OWN, c, buf["other0"])
            zrecv(FWD, c, buf["far0"])
            gather_stage(c)
            zcopy(WROW, c, buf["sw"], buf["w0"], end).start()
            zcopy(YROW, c, buf["sy"], buf["y0"], end).start()

        @pl.when(jnp.logical_and(hub, t >= nc + 1))
        def _():
            c = t - (nc + 1)
            here = jnp.where(c == nc - 2, 2, jnp.where(c == nc - 1, 1 if nc == 1 else 0, 1))

            def far_sum(e, carry):
                zrecv(SUM_F, e, buf["ba1"])
                end_sum_stage(e)
                zcopy(YEND, e, buf["se"], buf["y1"], end).start()
                return carry
            lax.fori_loop(c, c + here, far_sum, 0)

            @pl.when(c < nc - 1)
            def _():
                zrecv(SUM_O, c, buf["ba0"])
                own_sum_stage(c, "po", "ba0")

            @pl.when(c == nc - 1)
            def _():
                own_sum_stage(c, "po")
                for copy in held_copies():
                    copy.start()

        @pl.when(t == base_at)
        def _():
            from_whole_wait(BACK_K, buf["bk"])
            base_stage(s1, buf["bk"], wave.at[0], 1.0, 0)

        @pl.when(t == coupled_at)
        def _():
            @pl.when(jnp.logical_not(hub))
            def _():
                each_chunk(lambda c: zrecv(WROW, c, buf["w0"]))
            coupled_stage(buf["w0"], buf["w0b"])
            to_whole(TO_W0, buf["w0b"], buf["tw"])

        @pl.when(t == second_at)
        def _():
            to_whole_wait(TO_S0, buf["t0"])
            to_whole_wait(TO_W0, buf["tw"])
            first_stage([(buf["t0"], k1h, k1l), (buf["tw"], c1h, c1l)], buf["r0"])
            from_whole(BACK_0, buf["r0"], buf["b0"])

        @pl.when(t == last_at)
        def _():
            @pl.when(jnp.logical_not(hub))
            def _():
                each_chunk(lambda c: zrecv(YROW, c, buf["y0"]))
            from_whole_wait(BACK_0, buf["b0"])
            base_stage(s0, buf["b0"], wave.at[1], -1.0, 1, buf["y0"])
        return carry

    lax.fori_loop(0, 2 * nc + 1, body, 0)

    for kind, name in ((TO_S1, "s1b"), (BACK_C, "rc"), (BACK_K, "rk"), (TO_S0, "s0b"), (TO_W0, "w0b"), (BACK_0, "r0")):
        wide_sent(kind, buf[name])

    @pl.when(hub)
    def _():
        def sent(c):
            for kind, name in ((OWN, "s0"), (FWD, "end0"), (YROW, "sy"), (WROW, "sw"), (SUM_F, "af"), (YEND, "se")):
                zsent(kind, c, buf[name])

            @pl.when(c < nc - 1)
            def _():
                zsent(SUM_O, c, buf["ao"])
        each_chunk(sent)
        late_copy().wait()
        for copy in held_copies():
            copy.wait()
        last_near().wait_recv()
        tail = slice(rows - step, rows - late_rows)
        value = land[...]
        results[0, tail] = results[0, tail] + value
        results[2, tail] = results[2, tail] + half_step * value
        last_near().wait_send()

    @pl.when(jnp.logical_not(hub))
    def _():
        def sent(c):
            zsent(END, c, s0)
            zsent(PSI, c, s1)
            zsent(PHI, c, buf["phi"])
            zrecv(YEND, c, buf["y1"])
            own_sum_stage(c, "y1")
        each_chunk(sent)
        for copy in held_copies():
            copy.start()
        for n, matrix in enumerate((k2, c2)):
            end_matrix(n, matrix).wait_send()
        for copy in held_copies():
            copy.wait()


def write_kernel(results, slope_out, following_out, sems):
    ready = pl.ds(0, results.shape[1] - late_rows)
    copies = [
        pltpu.make_async_copy(results.at[0, ready], slope_out.at[0, ready], sems.at[0]),
        pltpu.make_async_copy(results.at[1], slope_out.at[1], sems.at[1]),
        pltpu.make_async_copy(results.at[2, ready], following_out.at[0, ready], sems.at[2]),
        pltpu.make_async_copy(results.at[3], following_out.at[1], sems.at[3]),
    ]
    for copy in copies:
        copy.start()
    for copy in copies:
        copy.wait()


def late_kernel(base, came, slope_in, following_in, slope_out, following_out, held, sems):
    at = pl.ds(slope_out.shape[1] - late_rows, late_rows)
    value = came[...]
    held[0] = base[0] + value
    held[1] = base[1] + half_step * value
    copies = [
        pltpu.make_async_copy(held.at[0], slope_out.at[0, at], sems.at[0]),
        pltpu.make_async_copy(held.at[1], following_out.at[0, at], sems.at[1]),
    ]
    for copy in copies:
        copy.start()
    for copy in copies:
        copy.wait()


def local(wide, wavefunction, previous_slope, potential, kinetic_one, coupling_one, kinetic_two, coupling_two, kinetic_three, coupling_three):
    _, rows, second, third = wavefunction.shape
    full = rows * wide
    q = second // wide
    shapes = []
    for name in BUFFERS:
        if name == "late":
            shape = (late_rows, second, third)
        elif name == "held":
            shape = (2, late_rows, second, third)
        elif name in WIDE_SHAPED:
            shape = (q, full, third)
        elif name in SECOND_FIRST:
            shape = (second, rows, third)
        else:
            shape = (rows, second, third)
        shapes.append(jax.ShapeDtypeStruct(shape, jnp.float32))
    shapes += [pltpu.VMEM((4, rows, second, third), jnp.float32)]
    nc = rows // 8
    bf = jnp.bfloat16
    everything = 4 * second
    outs = pl.pallas_call(
        functools.partial(kernel, wide),
        out_shape=shapes,
        in_specs=[pl.BlockSpec(memory_space=pl.ANY)] * 9,
        out_specs=[pl.BlockSpec(memory_space=pl.ANY)] * len(BUFFERS) + [pl.BlockSpec(memory_space=pltpu.VMEM)],
        scratch_shapes=[pltpu.VMEM((everything, everything), bf)] * 4
        + [pltpu.VMEM((full, full), bf)] * 4
        + [pltpu.VMEM((third, third), bf)] * 4
        + [
            pltpu.VMEM((everything, third), bf),
            pltpu.VMEM((everything, third), bf),
            pltpu.VMEM((4, second, third), jnp.float32),
            pltpu.VMEM((2, second, everything), jnp.float32),
            pltpu.VMEM((8 - late_rows, second, third), jnp.float32),
        ]
        + [pltpu.VMEM((second, everything), jnp.float32)] * 2
        + [pltpu.VMEM((full, full), jnp.float32)] * 2
        + [pltpu.VMEM((third, third), jnp.float32)] * 2
        + [
            pltpu.SemaphoreType.DMA((10, nc)),
            pltpu.SemaphoreType.DMA((10, nc)),
            pltpu.SemaphoreType.DMA((2,)),
            pltpu.SemaphoreType.DMA((2,)),
            pltpu.SemaphoreType.DMA((6,)),
            pltpu.SemaphoreType.DMA((3,)),
            pltpu.SemaphoreType.DMA((6,)),
            pltpu.SemaphoreType.DMA((6,)),
            pltpu.SemaphoreType.DMA((6,)),
        ],
        compiler_params=pltpu.CompilerParams(collective_id=0, has_side_effects=True, vmem_limit_bytes=26 * 2**20),
        cost_estimate=pl.CostEstimate(flops=6 * 3584 * 2 * rows * second * third * 2, bytes_accessed=40 * rows * second * third * 4, transcendentals=0),
    )(wavefunction, previous_slope, potential, kinetic_two, coupling_two, kinetic_one, coupling_one, kinetic_three, coupling_three)
    results = outs[len(BUFFERS)]
    came = lax.ppermute(outs[BUFFERS.index("late")], "narrow", [(1, 2), (2, 1)])
    shapes = [jax.ShapeDtypeStruct(wavefunction.shape, jnp.float32)] * 2
    whole = [pl.BlockSpec(memory_space=pl.ANY)] * 2
    written = pl.pallas_call(
        write_kernel,
        in_specs=[pl.BlockSpec(memory_space=pltpu.VMEM)],
        out_specs=whole,
        out_shape=shapes,
        scratch_shapes=[pltpu.SemaphoreType.DMA((4,))],
        compiler_params=pltpu.CompilerParams(vmem_limit_bytes=2**20),
        cost_estimate=pl.CostEstimate(flops=0, bytes_accessed=wavefunction.size * 8, transcendentals=0),
    )(results)
    return pl.pallas_call(
        late_kernel,
        in_specs=[pl.BlockSpec(memory_space=pltpu.VMEM)] * 2 + whole,
        out_specs=whole,
        out_shape=shapes,
        input_output_aliases={2: 0, 3: 1},
        scratch_shapes=[pltpu.VMEM((2, late_rows, second, third), jnp.float32), pltpu.SemaphoreType.DMA((2,))],
        compiler_params=pltpu.CompilerParams(vmem_limit_bytes=4 * 2**20),
        cost_estimate=pl.CostEstimate(flops=0, bytes_accessed=late_rows * second * third * 12, transcendentals=0),
    )(outs[BUFFERS.index("held")], came, *written)


def solution(mesh):
    wide = mesh.shape["wide"]
    field = P(None, "wide", "narrow", None)
    in_specs = (field, field, P("wide", "narrow", None), P(), P(), P("narrow", None), P("narrow", None), P(), P())

    def body(*arrays):
        return tuple(local(wide, *arrays))

    def run(*arrays):
        with jax.sharding.use_abstract_mesh(mesh.abstract_mesh):
            return jax.shard_map(body, mesh=mesh, in_specs=in_specs, out_specs=(field, field), check_vma=False)(*arrays)

    return run
```

```python
import functools

import jax
import jax.numpy as jnp
from jax import lax
from jax.experimental import pallas as pl
from jax.experimental.pallas import tpu as pltpu
from jax.sharding import PartitionSpec as P

half_step = 0.1
MESH = pl.DeviceIdType.MESH
OWN, END, FWD, YROW, WROW, PSI, PHI, SUM_O, SUM_F, YEND = range(10)
late_rows = 4
TO_S1, BACK_C, BACK_K, TO_S0, TO_W0, BACK_0 = range(6)
BUFFERS = (
    "end0", "other0", "far0", "y0", "w0", "sy", "sw",
    "s0b", "t0", "w0b", "tw", "r0", "b0",
    "s1b", "t1", "rc", "rk", "bc", "bk", "phi",
    "psie", "phie", "po", "pe", "ao", "af", "ba0", "ba1", "se", "y1", "s0", "s1", "late", "held",
)
WIDE_SHAPED = ("t0", "tw", "r0", "t1", "rc", "rk")
SECOND_FIRST = ("s0b", "w0b", "b0", "s1b", "bc", "bk")


def halves(x):
    high = x.astype(jnp.bfloat16)
    return high, (x - high.astype(jnp.float32)).astype(jnp.bfloat16)


def dot3(ah, al, bh, bl):
    dot = functools.partial(jnp.dot, preferred_element_type=jnp.float32)
    return dot(ah, bh) + dot(ah, bl) + dot(al, bh)


def kernel(wide, wave, prev, pot, k2, c2, k1, c1, k3, c3, *refs):
    buf = dict(zip(BUFFERS, refs[:len(BUFFERS)]))
    (results, wh, wl, wth, wtl, k1h, k1l, c1h, c1l, k3h, k3l, c3h, c3l, fh, fl, gather, wend, land,
     k2v, c2v, k1v, c1v, k3v, c3v, zs, zr, es, er, ms, ls, ws, wr, wloc) = refs[len(BUFFERS):]
    rows, second, third = wave.shape[1:]
    full = rows * wide
    q = second // wide
    step = 8
    nc = rows // step
    me = lax.axis_index("wide")
    z = lax.axis_index("narrow")
    hub = jnp.logical_or(z == 1, z == 2)
    end = jnp.where(z == 1, 0, 3)
    other = 3 - z
    far = 3 - end
    my_hub = jnp.where(z == 0, 1, 2)
    slope, following = results.at[pl.ds(0, 2)], results.at[pl.ds(2, 2)]
    s0, s1 = buf["s0"], buf["s1"]

    def peer_of(d):
        return lax.rem(me + d, wide)

    barrier = pltpu.get_barrier_semaphore()

    def greet(d, carry):
        pl.semaphore_signal(barrier, inc=1, device_id={"wide": peer_of(d)}, device_id_type=MESH)
        return carry

    lax.fori_loop(1, wide, greet, 0)

    @pl.when(hub)
    def _():
        pl.semaphore_signal(barrier, inc=1, device_id={"narrow": end}, device_id_type=MESH)
        pl.semaphore_signal(barrier, inc=1, device_id={"narrow": other}, device_id_type=MESH)

    @pl.when(jnp.logical_not(hub))
    def _():
        pl.semaphore_signal(barrier, inc=1, device_id={"narrow": my_hub}, device_id_type=MESH)

    def piece(ref, c):
        return ref.at[pl.ds(pl.multiple_of(c * step, step), step)]

    def zcopy(kind, c, src, dst, target):
        return pltpu.make_async_remote_copy(
            src_ref=piece(src, c), dst_ref=piece(dst, c), send_sem=zs.at[kind, c], recv_sem=zr.at[kind, c],
            device_id={"narrow": target}, device_id_type=MESH)

    def zrecv(kind, c, dst):
        pltpu.make_async_copy(piece(dst, c), piece(dst, c), zr.at[kind, c]).wait()

    def zsent(kind, c, src):
        pltpu.make_async_copy(piece(src, c), piece(src, c), zs.at[kind, c]).wait()

    def end_matrix(n, matrix):
        return pltpu.make_async_remote_copy(
            src_ref=matrix, dst_ref=wend.at[n], send_sem=es.at[n], recv_sem=er.at[n],
            device_id={"narrow": my_hub}, device_id_type=MESH)

    def last_near():
        return pltpu.make_async_remote_copy(
            src_ref=buf["ao"].at[pl.ds(rows - step, step - late_rows)], dst_ref=land, send_sem=zs.at[SUM_O, nc - 1],
            recv_sem=zr.at[SUM_O, nc - 1], device_id={"narrow": other}, device_id_type=MESH)

    def held_copies():
        late = pl.ds(rows - late_rows, late_rows)
        return [
            pltpu.make_async_copy(slope.at[0, late], buf["held"].at[0], ls.at[1]),
            pltpu.make_async_copy(following.at[0, late], buf["held"].at[1], ls.at[2]),
        ]

    def late_copy():
        return pltpu.make_async_copy(buf["ao"].at[pl.ds(rows - late_rows, late_rows)], buf["late"], ls.at[0])

    def each_chunk(f):
        def body(c, carry):
            f(c)
            return carry
        lax.fori_loop(0, nc, body, 0)

    def mine_of(ref, index, size):
        return ref.at[:, pl.ds(pl.multiple_of(index * size, size), size)]

    def to_whole(kind, src, dst):
        def send(d, carry):
            p = peer_of(d)
            pltpu.make_async_remote_copy(
                src_ref=src.at[pl.ds(p * q, q)], dst_ref=mine_of(dst, me, rows),
                send_sem=ws.at[kind], recv_sem=wr.at[kind], device_id={"wide": p}, device_id_type=MESH).start()
            return carry
        lax.fori_loop(1, wide, send, 0)
        pltpu.make_async_copy(src.at[pl.ds(me * q, q)], mine_of(dst, me, rows), wloc.at[kind]).start()

    def to_whole_wait(kind, dst):
        part = dst.at[:, pl.ds(0, (wide - 1) * rows)]
        pltpu.make_async_copy(part, part, wr.at[kind]).wait()
        own = dst.at[:, pl.ds(0, rows)]
        pltpu.make_async_copy(own, own, wloc.at[kind]).wait()

    def from_whole(kind, src, dst):
        def send(d, carry):
            p = peer_of(d)
            pltpu.make_async_remote_copy(
                src_ref=mine_of(src, p, rows), dst_ref=dst.at[pl.ds(me * q, q)],
                send_sem=ws.at[kind], recv_sem=wr.at[kind], device_id={"wide": p}, device_id_type=MESH).start()
            return carry
        lax.fori_loop(1, wide, send, 0)
        pltpu.make_async_copy(mine_of(src, me, rows), dst.at[pl.ds(me * q, q)], wloc.at[kind]).start()

    def from_whole_wait(kind, dst):
        part = dst.at[pl.ds(0, (wide - 1) * q)]
        pltpu.make_async_copy(part, part, wr.at[kind]).wait()
        own = dst.at[pl.ds(0, q)]
        pltpu.make_async_copy(own, own, wloc.at[kind]).wait()

    def wide_sent(kind, src):
        part = src.at[pl.ds(0, (wide - 1) * q)] if src.shape[0] == second else src.at[:, pl.ds(0, (wide - 1) * rows)]
        pltpu.make_async_copy(part, part, ws.at[kind]).wait()

    by_first = pl.BlockSpec((step, second, third), lambda i: (i, 0, 0))
    by_second = pl.BlockSpec((second, step, third), lambda i: (0, i, 0))
    one_row = pl.BlockSpec((1, second, third), lambda i: (i, 0, 0))
    one_whole = pl.BlockSpec((1, full, third), lambda i: (i, 0, 0))

    parts = 2
    half_first = pl.BlockSpec((step, second // parts, third), lambda i, j: (i, j, 0))
    half_second = pl.BlockSpec((second // parts, step, third), lambda i, j: (j, i, 0))
    quarter = pl.BlockSpec((step // 2, second, third), lambda i: (i, 0, 0))

    def transpose_stage(src, dst):
        def body(x, out):
            for g in range(second // 8):
                out[8 * g:8 * g + 8, :, :] = jnp.swapaxes(x[:, 8 * g:8 * g + 8, :], 0, 1)
        pltpu.emit_pipeline(body, grid=(nc,), in_specs=[by_first], out_specs=[by_second])(src, dst)

    def section_stage(start, size, block):
        spec = pl.BlockSpec((block, second, third), lambda i: (i, 0, 0))

        def body(x, y, out):
            out[...] = x[...] + half_step * y[...]
        cut = pl.ds(start, size)
        pltpu.emit_pipeline(body, grid=(size // block,), in_specs=[spec] * 2, out_specs=[spec])(
            wave.at[0, cut], prev.at[0, cut], s0.at[cut])

    def section_swapped_stage():
        def body(x, y, out, out_swapped):
            for g in range(second // 8):
                cut = slice(8 * g, 8 * g + 8)
                value = x[:, cut, :] + half_step * y[:, cut, :]
                out[:, cut, :] = value
                out_swapped[cut, :, :] = jnp.swapaxes(value, 0, 1)
        pltpu.emit_pipeline(body, grid=(nc,), in_specs=[by_first] * 2, out_specs=[by_first, by_second])(
            wave.at[1], prev.at[1], s1, buf["s1b"])

    def third_dot(x, mh, ml):
        xh, xl = halves(x)
        return dot3(xh, xl, mh[...], ml[...])

    group = 32

    def phi_stage(src, dst):
        def body(x, out):
            for g in range(second // group):
                block = x[group * g:group * (g + 1)].reshape(group * step, third)
                result = third_dot(block, c3h, c3l).reshape(group, step, third)
                out[:, group * g:group * (g + 1), :] = jnp.swapaxes(result, 0, 1)
        pltpu.emit_pipeline(body, grid=(nc,), in_specs=[by_second], out_specs=[by_first])(src, dst)

    def coupled_stage(src, dst):
        def body(x, out):
            for g in range(second // group):
                block = x[:, group * g:group * (g + 1), :].reshape(group * step, third)
                result = third_dot(block, c3h, c3l).reshape(step, group, third)
                out[group * g:group * (g + 1), :, :] = jnp.swapaxes(result, 0, 1)
        pltpu.emit_pipeline(body, grid=(nc,), in_specs=[by_first], out_specs=[by_second])(src, dst)

    def base_stage(field, returned, start, sign, slot, extra=None):
        def body(x, v, back, base, *rest):
            out, out_next = rest[-2:]
            for g in range(second // parts // group):
                cut = slice(group * g, group * (g + 1))
                block = x[:, cut, :].reshape(group * step, third)
                result = third_dot(block, k3h, k3l).reshape(step, group, third)
                result = result + v[:, cut, :] * x[:, cut, :] + jnp.swapaxes(back[cut], 0, 1)
                if extra is not None:
                    result = result + rest[0][:, cut, :]
                result = sign * result
                out[:, cut, :] = result
                out_next[:, cut, :] = base[:, cut, :] + half_step * result
        ins = [field, pot, returned, start] + ([] if extra is None else [extra])
        specs = [half_first, half_first, half_second, half_first] + ([] if extra is None else [half_first])
        pltpu.emit_pipeline(body, grid=(nc, parts), in_specs=specs, out_specs=[half_first] * 2)(
            *ins, slope.at[slot], following.at[slot])

    def first_stage(terms, dst):
        def body(*args):
            out = args[-1]
            total = None
            for (_, mh, ml), x in zip(terms, args[:-1]):
                xh, xl = halves(x[0])
                value = dot3(mh[...], ml[...], xh, xl)
                total = value if total is None else total + value
            out[0] = total
        pltpu.emit_pipeline(body, grid=(q,), in_specs=[one_whole] * len(terms), out_specs=[one_whole])(
            *[t[0] for t in terms], dst)

    def place(slot, x):
        at = pl.ds(pl.multiple_of(slot * second, second), second)
        high, low = halves(x)
        fh[at, :] = high
        fl[at, :] = low

    def gather_stage(c):
        def body(own, e, o, f, y, v, ye, ve):
            place(z, own[0])
            place(end, e[0])
            place(other, o[0])
            place(far, f[0])
            for n, out in enumerate((y, ye, v, ve)):
                cut = slice(n * second, (n + 1) * second)
                out[0] = dot3(wh[cut, :], wl[cut, :], fh[...], fl[...])
        pltpu.emit_pipeline(body, grid=(step,), in_specs=[one_row] * 4, out_specs=[one_row] * 4)(
            piece(s0, c), piece(buf["end0"], c), piece(buf["other0"], c), piece(buf["far0"], c),
            piece(buf["y0"], c), piece(buf["w0"], c), piece(buf["sy"], c), piece(buf["sw"], c))

    def scatter_stage(c):
        def body(own, e, pown, pend, yo, ye, ao, af):
            place(0, own[0])
            place(1, e[0])
            place(2, pown[0])
            place(3, pend[0])
            for n in range(4):
                cut = slice(n * second, (n + 1) * second)
                gather[n] = dot3(wth[cut, :], wtl[cut, :], fh[...], fl[...])
            yo[0] = gather[z]
            ye[0] = gather[end]
            ao[0] = gather[other]
            af[0] = gather[far]
        pltpu.emit_pipeline(body, grid=(step,), in_specs=[one_row] * 4, out_specs=[one_row] * 4)(
            piece(s1, c), piece(buf["psie"], c), piece(buf["phi"], c), piece(buf["phie"], c),
            piece(buf["po"], c), piece(buf["pe"], c), piece(buf["ao"], c), piece(buf["af"], c))

    def end_sum_stage(c):
        def body(x, y, out):
            out[...] = x[...] + y[...]
        pltpu.emit_pipeline(body, grid=(2,), in_specs=[quarter] * 2, out_specs=[quarter])(
            piece(buf["pe"], c), piece(buf["ba1"], c), piece(buf["se"], c))

    def own_sum_stage(c, *terms):
        def body(*args):
            value = args[0][...]
            for term in args[1:-2]:
                value = value + term[...]
            args[-2][...] += value
            args[-1][...] += half_step * value
        pltpu.emit_pipeline(body, grid=(2,), in_specs=[quarter] * len(terms), out_specs=[quarter] * 2)(
            *[piece(buf[term], c) for term in terms], piece(slope.at[0], c), piece(following.at[0], c))

    ahead = min(3, nc)
    small = step // 4

    def first_piece(i):
        at = pl.ds(i * small, small)
        pltpu.make_async_remote_copy(
            src_ref=s0.at[at], dst_ref=buf["other0"].at[at], send_sem=zs.at[OWN, 0], recv_sem=zr.at[OWN, 0],
            device_id={"narrow": other}, device_id_type=MESH).start()

    section_stage(0, small, small)

    @pl.when(hub)
    def _():
        pl.semaphore_wait(barrier, wide + 1)
        first_piece(0)

    @pl.when(jnp.logical_not(hub))
    def _():
        pl.semaphore_wait(barrier, wide)

    def next_piece(i, carry):
        section_stage(i * small, small, small)

        @pl.when(hub)
        def _():
            first_piece(i)
        return carry
    lax.fori_loop(1, step // small, next_piece, 0)

    @pl.when(jnp.logical_not(hub))
    def _():
        zcopy(END, 0, s0, buf["end0"], my_hub).start()
        for n, matrix in enumerate((k2, c2)):
            end_matrix(n, matrix).start()

    fetches = [
        pltpu.make_async_copy(matrix, held, ms.at[n])
        for n, (matrix, held) in enumerate(((k2, k2v), (c2, c2v), (k1, k1v), (c1, c1v), (k3, k3v), (c3, c3v)))
    ]
    for fetch in fetches:
        fetch.start()

    if nc > 1:
        section_stage(step, rows - step, step // 2)

        @pl.when(hub)
        def _():
            for c in range(1, ahead):
                zcopy(OWN, c, s0, buf["other0"], other).start()

        @pl.when(jnp.logical_not(hub))
        def _():
            for c in range(1, nc):
                zcopy(END, c, s0, buf["end0"], my_hub).start()

    section_swapped_stage()
    to_whole(TO_S1, buf["s1b"], buf["t1"])
    for fetch in fetches:
        fetch.wait()
    for matrix, high, low in ((c1v, c1h, c1l), (c3v, c3h, c3l), (k1v, k1h, k1l), (k3v, k3h, k3l)):
        high[...], low[...] = halves(matrix[...])

    @pl.when(hub)
    def _():
        for n, (matrix, held) in enumerate(((k2, k2v), (c2, c2v))):
            end_matrix(n, matrix).wait_recv()
            for m, rows_of in enumerate((held, wend.at[n])):
                cut = slice((2 * n + m) * second, (2 * n + m + 1) * second)
                value = rows_of[...]
                wh[cut, :], wl[cut, :] = halves(value)
                wth[:, cut], wtl[:, cut] = halves(value.T)

    first_at = min(3, nc - 1)
    phi_at = min(5, nc - 1)
    base_at = nc
    coupled_at = nc + 1
    second_at = min(nc + 4, 2 * nc)
    last_at = max(2 * nc - 2, second_at)
    early = nc // 2

    def body(t, carry):
        @pl.when(jnp.logical_and(hub, t + ahead < nc))
        def _():
            zcopy(OWN, t + ahead, s0, buf["other0"], other).start()

        @pl.when(jnp.logical_and(hub, t < nc))
        def _():
            zrecv(END, t, buf["end0"])
            zcopy(FWD, t, buf["end0"], buf["far0"], other).start()

        @pl.when(t == first_at)
        def _():
            to_whole_wait(TO_S1, buf["t1"])
            first_stage([(buf["t1"], c1h, c1l)], buf["rc"])
            from_whole(BACK_C, buf["rc"], buf["bc"])

            @pl.when(jnp.logical_not(hub))
            def _():
                for c in range(early):
                    zcopy(PSI, c, s1, buf["psie"], my_hub).start()
            first_stage([(buf["t1"], k1h, k1l)], buf["rk"])
            transpose_stage(s0, buf["s0b"])

        @pl.when(t == phi_at)
        def _():
            from_whole_wait(BACK_C, buf["bc"])
            phi_stage(buf["bc"], buf["phi"])

            @pl.when(jnp.logical_not(hub))
            def _():
                for c in range(nc):
                    if c >= early:
                        zcopy(PSI, c, s1, buf["psie"], my_hub).start()
                    zcopy(PHI, c, buf["phi"], buf["phie"], my_hub).start()
            from_whole(BACK_K, buf["rk"], buf["bk"])
            to_whole(TO_S0, buf["s0b"], buf["t0"])

        @pl.when(jnp.logical_and(hub, jnp.logical_and(t >= nc - 1, t <= 2 * nc - 2)))
        def _():
            c = t - (nc - 1)
            zrecv(PSI, c, buf["psie"])
            zrecv(PHI, c, buf["phie"])
            scatter_stage(c)
            zcopy(SUM_F, c, buf["af"], buf["ba1"], other).start()

            if nc == 1:
                last_near().start()
                late_copy().start()

            @pl.when(c < nc - 2)
            def _():
                zcopy(SUM_O, c, buf["ao"], buf["ba0"], other).start()

        @pl.when(jnp.logical_and(hub, jnp.logical_and(t >= 1, t <= nc)))
        def _():
            c = t - 1
            zrecv(OWN, c, buf["other0"])
            zrecv(FWD, c, buf["far0"])
            gather_stage(c)
            zcopy(WROW, c, buf["sw"], buf["w0"], end).start()
            zcopy(YROW, c, buf["sy"], buf["y0"], end).start()

        @pl.when(jnp.logical_and(hub, t >= nc + 1))
        def _():
            c = t - (nc + 1)
            here = jnp.where(c == nc - 2, 2, jnp.where(c == nc - 1, 1 if nc == 1 else 0, 1))

            def far_sum(e, carry):
                zrecv(SUM_F, e, buf["ba1"])
                end_sum_stage(e)
                zcopy(YEND, e, buf["se"], buf["y1"], end).start()
                return carry

            @pl.when(c == nc - 2)
            def _():
                zcopy(SUM_O, c, buf["ao"], buf["ba0"], other).start()
            lax.fori_loop(c, c + here, far_sum, 0)

            @pl.when(c == nc - 2)
            def _():
                last_near().start()
                late_copy().start()

            @pl.when(c < nc - 1)
            def _():
                zrecv(SUM_O, c, buf["ba0"])
                own_sum_stage(c, "po", "ba0")

            @pl.when(c == nc - 1)
            def _():
                own_sum_stage(c, "po")
                for copy in held_copies():
                    copy.start()

        @pl.when(t == base_at)
        def _():
            from_whole_wait(BACK_K, buf["bk"])
            base_stage(s1, buf["bk"], wave.at[0], 1.0, 0)

        @pl.when(t == coupled_at)
        def _():
            @pl.when(jnp.logical_not(hub))
            def _():
                each_chunk(lambda c: zrecv(WROW, c, buf["w0"]))
            coupled_stage(buf["w0"], buf["w0b"])
            to_whole(TO_W0, buf["w0b"], buf["tw"])

        @pl.when(t == second_at)
        def _():
            to_whole_wait(TO_S0, buf["t0"])
            to_whole_wait(TO_W0, buf["tw"])
            first_stage([(buf["t0"], k1h, k1l), (buf["tw"], c1h, c1l)], buf["r0"])
            from_whole(BACK_0, buf["r0"], buf["b0"])

        @pl.when(t == last_at)
        def _():
            @pl.when(jnp.logical_not(hub))
            def _():
                each_chunk(lambda c: zrecv(YROW, c, buf["y0"]))
            from_whole_wait(BACK_0, buf["b0"])
            base_stage(s0, buf["b0"], wave.at[1], -1.0, 1, buf["y0"])
        return carry

    lax.fori_loop(0, 2 * nc + 1, body, 0)

    for kind, name in ((TO_S1, "s1b"), (BACK_C, "rc"), (BACK_K, "rk"), (TO_S0, "s0b"), (TO_W0, "w0b"), (BACK_0, "r0")):
        wide_sent(kind, buf[name])

    @pl.when(hub)
    def _():
        def sent(c):
            for kind, name in ((OWN, "s0"), (FWD, "end0"), (YROW, "sy"), (WROW, "sw"), (SUM_F, "af"), (YEND, "se")):
                zsent(kind, c, buf[name])

            @pl.when(c < nc - 1)
            def _():
                zsent(SUM_O, c, buf["ao"])
        each_chunk(sent)
        late_copy().wait()
        for copy in held_copies():
            copy.wait()
        last_near().wait_recv()
        tail = slice(rows - step, rows - late_rows)
        value = land[...]
        results[0, tail] = results[0, tail] + value
        results[2, tail] = results[2, tail] + half_step * value
        last_near().wait_send()

    @pl.when(jnp.logical_not(hub))
    def _():
        def sent(c):
            zsent(END, c, s0)
            zsent(PSI, c, s1)
            zsent(PHI, c, buf["phi"])
            zrecv(YEND, c, buf["y1"])
            own_sum_stage(c, "y1")
        each_chunk(sent)
        for copy in held_copies():
            copy.start()
        for n, matrix in enumerate((k2, c2)):
            end_matrix(n, matrix).wait_send()
        for copy in held_copies():
            copy.wait()


def write_kernel(results, slope_out, following_out, sems):
    ready = pl.ds(0, results.shape[1] - late_rows)
    copies = [
        pltpu.make_async_copy(results.at[0, ready], slope_out.at[0, ready], sems.at[0]),
        pltpu.make_async_copy(results.at[1], slope_out.at[1], sems.at[1]),
        pltpu.make_async_copy(results.at[2, ready], following_out.at[0, ready], sems.at[2]),
        pltpu.make_async_copy(results.at[3], following_out.at[1], sems.at[3]),
    ]
    for copy in copies:
        copy.start()
    for copy in copies:
        copy.wait()


def late_kernel(base, came, slope_in, following_in, slope_out, following_out, held, sems):
    at = pl.ds(slope_out.shape[1] - late_rows, late_rows)
    value = came[...]
    held[0] = base[0] + value
    held[1] = base[1] + half_step * value
    copies = [
        pltpu.make_async_copy(held.at[0], slope_out.at[0, at], sems.at[0]),
        pltpu.make_async_copy(held.at[1], following_out.at[0, at], sems.at[1]),
    ]
    for copy in copies:
        copy.start()
    for copy in copies:
        copy.wait()


def local(wide, wavefunction, previous_slope, potential, kinetic_one, coupling_one, kinetic_two, coupling_two, kinetic_three, coupling_three):
    _, rows, second, third = wavefunction.shape
    full = rows * wide
    q = second // wide
    shapes = []
    for name in BUFFERS:
        if name == "late":
            shape = (late_rows, second, third)
        elif name == "held":
            shape = (2, late_rows, second, third)
        elif name in WIDE_SHAPED:
            shape = (q, full, third)
        elif name in SECOND_FIRST:
            shape = (second, rows, third)
        else:
            shape = (rows, second, third)
        shapes.append(jax.ShapeDtypeStruct(shape, jnp.float32))
    shapes += [pltpu.VMEM((4, rows, second, third), jnp.float32)]
    nc = rows // 8
    bf = jnp.bfloat16
    everything = 4 * second
    outs = pl.pallas_call(
        functools.partial(kernel, wide),
        out_shape=shapes,
        in_specs=[pl.BlockSpec(memory_space=pl.ANY)] * 9,
        out_specs=[pl.BlockSpec(memory_space=pl.ANY)] * len(BUFFERS) + [pl.BlockSpec(memory_space=pltpu.VMEM)],
        scratch_shapes=[pltpu.VMEM((everything, everything), bf)] * 4
        + [pltpu.VMEM((full, full), bf)] * 4
        + [pltpu.VMEM((third, third), bf)] * 4
        + [
            pltpu.VMEM((everything, third), bf),
            pltpu.VMEM((everything, third), bf),
            pltpu.VMEM((4, second, third), jnp.float32),
            pltpu.VMEM((2, second, everything), jnp.float32),
            pltpu.VMEM((8 - late_rows, second, third), jnp.float32),
        ]
        + [pltpu.VMEM((second, everything), jnp.float32)] * 2
        + [pltpu.VMEM((full, full), jnp.float32)] * 2
        + [pltpu.VMEM((third, third), jnp.float32)] * 2
        + [
            pltpu.SemaphoreType.DMA((10, nc)),
            pltpu.SemaphoreType.DMA((10, nc)),
            pltpu.SemaphoreType.DMA((2,)),
            pltpu.SemaphoreType.DMA((2,)),
            pltpu.SemaphoreType.DMA((6,)),
            pltpu.SemaphoreType.DMA((3,)),
            pltpu.SemaphoreType.DMA((6,)),
            pltpu.SemaphoreType.DMA((6,)),
            pltpu.SemaphoreType.DMA((6,)),
        ],
        compiler_params=pltpu.CompilerParams(collective_id=0, has_side_effects=True, vmem_limit_bytes=26 * 2**20),
        cost_estimate=pl.CostEstimate(flops=6 * 3584 * 2 * rows * second * third * 2, bytes_accessed=40 * rows * second * third * 4, transcendentals=0),
    )(wavefunction, previous_slope, potential, kinetic_two, coupling_two, kinetic_one, coupling_one, kinetic_three, coupling_three)
    results = outs[len(BUFFERS)]
    came = lax.ppermute(outs[BUFFERS.index("late")], "narrow", [(1, 2), (2, 1)])
    shapes = [jax.ShapeDtypeStruct(wavefunction.shape, jnp.float32)] * 2
    whole = [pl.BlockSpec(memory_space=pl.ANY)] * 2
    written = pl.pallas_call(
        write_kernel,
        in_specs=[pl.BlockSpec(memory_space=pltpu.VMEM)],
        out_specs=whole,
        out_shape=shapes,
        scratch_shapes=[pltpu.SemaphoreType.DMA((4,))],
        compiler_params=pltpu.CompilerParams(vmem_limit_bytes=2**20),
        cost_estimate=pl.CostEstimate(flops=0, bytes_accessed=wavefunction.size * 8, transcendentals=0),
    )(results)
    return pl.pallas_call(
        late_kernel,
        in_specs=[pl.BlockSpec(memory_space=pltpu.VMEM)] * 2 + whole,
        out_specs=whole,
        out_shape=shapes,
        input_output_aliases={2: 0, 3: 1},
        scratch_shapes=[pltpu.VMEM((2, late_rows, second, third), jnp.float32), pltpu.SemaphoreType.DMA((2,))],
        compiler_params=pltpu.CompilerParams(vmem_limit_bytes=4 * 2**20),
        cost_estimate=pl.CostEstimate(flops=0, bytes_accessed=late_rows * second * third * 12, transcendentals=0),
    )(outs[BUFFERS.index("held")], came, *written)


def solution(mesh):
    wide = mesh.shape["wide"]
    field = P(None, "wide", "narrow", None)
    in_specs = (field, field, P("wide", "narrow", None), P(), P(), P("narrow", None), P("narrow", None), P(), P())

    def body(*arrays):
        return tuple(local(wide, *arrays))

    def run(*arrays):
        with jax.sharding.use_abstract_mesh(mesh.abstract_mesh):
            return jax.shard_map(body, mesh=mesh, in_specs=in_specs, out_specs=(field, field), check_vma=False)(*arrays)

    return run
```
